32 devices in a mesh: parts: 2 (over x), blk: 16 (over z, y, core).
Axes of the slice: x: 2, y: 2, z: 4, core: 2. Of those that a mesh axis runs over, the one named last changes fastest.
Arguments:
- observed: bfloat16 [24576, 1024], P(('parts', 'blk')), parts along dimension 0, may hold values from -6 to 6
- sharpness: float32 [24576], P(('parts', 'blk')), parts along dimension 0, may hold values from 0.03 to 0.15
- obs_class: int32 [24576], P(('parts', 'blk')), parts along dimension 0, may hold values from 0 to 7
- pattern: int32 [192, 16], P(('parts', 'blk')), parts along dimension 0, may hold values from 0 to 1, as said below
- evolved: bfloat16 [4096, 1024], P(('parts', 'blk')), parts along dimension 0, may hold values from -6 to 6
- sim_params: bfloat16 [4, 4096], P(None, ('parts', 'blk')), parts along dimension 1, may hold values from -6 to 6
- sim_class: int32 [4096], P(('parts', 'blk')), parts along dimension 0, may hold values from 0 to 7, as said below
Outputs:
- posterior_mean: float32 [4, 24576], P(None, ('parts', 'blk')), parts along dimension 1
- log_evidence: float32 [24576], P(('parts', 'blk')), parts along dimension 0
The draws below stay inside these ranges and needn't reach their ends.
There are 2 independent parts, one for each index of `parts`. The reference program is written for one: setup_inputs(seed, part) draws one part's arguments, and reference() takes and returns one part's arrays. A program takes and returns all parts, laid end to end along the dimension named above; each array names one. Nothing has to cross between parts.
Inputs may be any that keep to these rules, and one draw needn't show every extreme that they name: `sim_class`: every block of 128 evolved profiles holds every class, at its first 8 positions. `pattern`: every block of observed profiles is compared with at least one block of evolved profiles; the share of compared blocks differs from one observed block to another.
All inputs are finite; a program needn't handle non-finite values.
Results may differ from the reference program's by a relative error of at most 0.0045.
Values may be sent and summed in bfloat16 or wider, within the bound.
No kernel may reach another device: no remote copies, remote signals or barrier semaphores. Data moves between devices by JAX's collectives and lax.ppermute only.
A program may use at most 64 MiB of HBM per device.

```python
import math
import jax
import jax.numpy as jnp
from jax import lax

P_SIZE = 1024
NPARAM = 4
NCLASS = 8
BLOCK = 128
NOBS = 12288
NSIM = 2048
OBS_BLOCKS = 96
SIM_BLOCKS = 16


def class_tables(key):
    key_sim = jax.random.fold_in(key, 101)
    key_obs = jax.random.fold_in(key, 102)
    key_level = jax.random.fold_in(key, 103)
    key_mask = jax.random.fold_in(key, 104)
    key_force = jax.random.fold_in(key, 105)
    sim_class = jax.random.randint(key_sim, (NSIM,), 0, NCLASS)
    within = jnp.arange(NSIM) % BLOCK
    sim_class = jnp.where(within < NCLASS, within, sim_class).astype(jnp.int32)
    obs_class = jax.random.randint(key_obs, (NOBS,), 0, NCLASS).astype(jnp.int32)
    levels = jax.random.randint(key_level, (OBS_BLOCKS, 1), 1, 9)
    rolls = jax.random.randint(key_mask, (OBS_BLOCKS, SIM_BLOCKS), 0, 16)
    forced = jax.random.randint(key_force, (OBS_BLOCKS, 1), 0, SIM_BLOCKS)
    opened = (rolls < levels) | (jnp.arange(SIM_BLOCKS)[None, :] == forced)
    return (obs_class, sim_class, opened.astype(jnp.int32))


def sim_values(key):
    key_base = jax.random.fold_in(key, 201)
    base = jax.random.normal(key_base, (NSIM, P_SIZE), jnp.float32)
    return jnp.clip(base, -6.0, 6.0)


def draw_obs_class(key, part):
    return class_tables(key)[0]


def draw_sim_class(key, part):
    return class_tables(key)[1]


def draw_pattern(key, part):
    return class_tables(key)[2]


def draw_evolved(key, part):
    return sim_values(key).astype(jnp.bfloat16)


def draw_observed(key, part):
    key_own = jax.random.fold_in(key, 301)
    base = jax.random.normal(key_own, (NOBS, P_SIZE), jnp.float32)
    return jnp.clip(base, -6.0, 6.0).astype(jnp.bfloat16)


def block_levels(rng, shape, shards, least, largest):
    factor_of = 1.0
    for dim, blocks in shards:
        draws = jax.random.uniform(jax.random.fold_in(jax.random.fold_in(rng, 6), dim), (blocks,), jnp.float32, least / len(shards), largest / len(shards))
        factor_of = factor_of * jnp.repeat(jnp.exp(draws), shape[dim] // blocks).reshape((-1,) + (1,) * (len(shape) - 1 - dim))
    return factor_of


def gaussian(key, dims, spread, limit, shards=(), held_as=jnp.bfloat16):
    gain = block_levels(key, dims, shards, -0.22, 0.18) if shards else 1.0
    array = jax.random.normal(key, dims, jnp.float32) * spread * gain
    return jnp.minimum(jnp.maximum(array, -limit), limit).astype(held_as)


def setup_inputs(seed: int = 0, part: int = 0) -> dict:
    splits = jax.random.split(jax.random.key(seed), 8)
    part_keys = jax.random.split(jax.random.fold_in(splits[7], part), 8)
    observed = draw_observed(jax.random.fold_in(jax.random.fold_in(splits[7], part), 71), part)
    sharpness = jnp.clip(jnp.exp(math.log(0.15) - 1.609438 * jax.random.uniform(part_keys[1], (NOBS,), jnp.float32) ** block_levels(part_keys[1], (NOBS,), ((0, 16),), -0.2, 0.2)), 0.03, 0.15)
    obs_class = draw_obs_class(jax.random.fold_in(jax.random.fold_in(splits[7], part), 71), part)
    pattern = draw_pattern(jax.random.fold_in(jax.random.fold_in(splits[7], part), 71), part)
    evolved = draw_evolved(jax.random.fold_in(jax.random.fold_in(splits[7], part), 71), part)
    sim_params = gaussian(part_keys[5], (NPARAM, NSIM), 1.0, 6.0, ((1, 16),))
    sim_class = draw_sim_class(jax.random.fold_in(jax.random.fold_in(splits[7], part), 71), part)
    return dict(observed=observed, sharpness=sharpness, obs_class=obs_class, pattern=pattern, evolved=evolved, sim_params=sim_params, sim_class=sim_class)


NEG_START = -1.0e30


def visit_block(observed, obs_sq, sharpness, obs_class, rows_open, sims, params, sims_class, running_max, weight_total, param_sums):
    sims_sq = jnp.sum(jnp.square(sims.astype(jnp.float32)), axis=1)
    inner = lax.dot_general(observed, sims, (((1,), (1,)), ((), ())), preferred_element_type=jnp.float32)
    distance = obs_sq[:, None] + sims_sq[None, :] - 2.0 * inner
    score = sharpness[:, None] * (2.0 * P_SIZE - distance)
    active = rows_open[:, None] & (obs_class[:, None] == sims_class[None, :])
    new_max = jnp.maximum(running_max, jnp.max(jnp.where(active, score, NEG_START), axis=1))
    factor = jnp.exp(running_max - new_max)
    weights = jnp.where(active, jnp.exp(score - new_max[:, None]), 0.0)
    weight_total = weight_total * factor + jnp.sum(weights, axis=1)
    weight_low = weights.astype(jnp.bfloat16)
    added = lax.dot_general(params, weight_low, (((1,), (1,)), ((), ())), preferred_element_type=jnp.float32)
    param_sums = param_sums * factor[None, :] + added
    return new_max, weight_total, param_sums


def reference(observed, sharpness, obs_class, pattern, evolved, sim_params, sim_class):
    obs_sq = jnp.sum(jnp.square(observed.astype(jnp.float32)), axis=1)
    row_block = (jnp.arange(NOBS) // BLOCK).astype(jnp.int32)
    sims_all = evolved.reshape(SIM_BLOCKS, BLOCK, P_SIZE)
    params_all = jnp.transpose(sim_params.reshape(NPARAM, SIM_BLOCKS, BLOCK), (1, 0, 2))
    class_all = sim_class.reshape(SIM_BLOCKS, BLOCK)
    block_ids = jnp.arange(SIM_BLOCKS).astype(jnp.int32)

    def step(carry, inputs):
        sims, params, sims_class, block_id = inputs
        column = lax.dynamic_slice_in_dim(pattern, block_id, 1, 1)[:, 0]
        rows_open = column[row_block] == 1
        result = visit_block(observed, obs_sq, sharpness, obs_class, rows_open, sims, params, sims_class, carry[0], carry[1], carry[2])
        return result, None

    start = (jnp.full((NOBS,), NEG_START, jnp.float32), jnp.zeros((NOBS,), jnp.float32), jnp.zeros((NPARAM, NOBS), jnp.float32))
    final, _ = lax.scan(step, start, (sims_all, params_all, class_all, block_ids))
    running_max, weight_total, param_sums = final
    return param_sums / weight_total[None, :], running_max + jnp.log(weight_total)
```

```python
import functools
import math

import jax
import jax.numpy as jnp
from jax import lax
from jax.experimental import pallas as pl
from jax.experimental.pallas import tpu as pltpu
from jax.sharding import PartitionSpec as P

NEG_START = -1e30
LOG2E = math.log2(math.e)
LANES = 256
SUBLANES = 8
VMEM_LIMIT = 40 * 1024 * 1024


def ring_of(chips, grid):
    if grid and chips % 2 == 0:
        return [2 * z for z in range(chips // 2)] + [2 * z + 1 for z in reversed(range(chips // 2))]
    return list(range(chips))


def plan(size, grid):
    chips = size // 2
    ring = ring_of(chips, grid)
    place = {chip: at for at, chip in enumerate(ring)}

    def beside(device, by):
        return ring[(place[device // 2] + by) % chips] * 2 + device % 2

    ways = [[1 if device % 2 == kind else -1 for device in range(size)] for kind in range(2)]
    pairs = [[(device, beside(device, ways[kind][device])) for device in range(size)] for kind in range(2)]
    order = [
        [device] + [beside(device, -ways[step % 2][device] * (step // 2 + 1)) for step in range(chips - 1)]
        for device in range(size)
    ]
    return pairs, order


def row(values):
    return values.reshape(1, values.shape[-1])


def prepare_kernel(
    at_ref, order_ref, pattern_ref, class_ref, sharp_ref, observed_ref, params_ref, sim_class_ref,
    own_ref, sib_ref, meta_ref, square_ref,
):
    steps = order_ref.shape[1]
    tiles = pattern_ref.shape[0]
    rows = class_ref.shape[-1]
    tile = rows // tiles
    at = at_ref[0]
    classes = row(class_ref[...]).astype(jnp.float32)
    scale = row(sharp_ref[...]) * (2.0 * LOG2E)
    own_ref[...] = jnp.zeros_like(own_ref)
    sib_ref[...] = jnp.zeros_like(sib_ref)
    own_ref[0:1, :] = scale
    sib_ref[0:1, :] = scale
    for step in range(steps):
        for out_ref, device in ((own_ref, at), (sib_ref, at ^ 1)):
            block = order_ref[device, step]
            for i in range(tiles):
                columns = slice(i * tile, (i + 1) * tile)
                is_open = pattern_ref[i, block] == 1
                out_ref[step + 1 : step + 2, columns] = jnp.where(is_open, classes[:, columns], -1.0)
    meta_ref[...] = jnp.zeros_like(meta_ref)
    meta_ref[0 : params_ref.shape[0], :] = params_ref[...].astype(jnp.float32)
    meta_ref[SUBLANES - 1 : SUBLANES, :] = row(sim_class_ref[...]).astype(jnp.float32)
    ones = jnp.ones((SUBLANES, observed_ref.shape[1]), jnp.bfloat16)
    for i in range(rows // LANES):
        part = observed_ref[i * LANES : (i + 1) * LANES, :].astype(jnp.float32)
        square = part * part
        high = square.astype(jnp.bfloat16)
        low = (square - high.astype(jnp.float32)).astype(jnp.bfloat16)
        total = lax.dot_general(ones, high, (((1,), (1,)), ((), ())), preferred_element_type=jnp.float32)
        total += lax.dot_general(ones, low, (((1,), (1,)), ((), ())), preferred_element_type=jnp.float32)
        square_ref[:, i * LANES : (i + 1) * LANES] = total


def absorb_kernel(step, own_ref, sib_ref, own_aux_ref, sib_aux_ref, block_ref, meta_ref, state_ref, out_ref):
    block = block_ref[...]
    wide = block.astype(jnp.float32)
    half_square = 0.5 * jnp.sum(wide * wide, axis=1, keepdims=True)
    meta = meta_ref[...]
    params = meta.astype(jnp.bfloat16)
    count = meta.shape[1]
    square_meta = jnp.concatenate([meta] + [jnp.zeros_like(meta)] * (count // SUBLANES - 1), axis=0)
    sim_class = square_meta.T[:, SUBLANES - 1 : SUBLANES]
    rows = own_ref.shape[0]
    for half, (obs_ref, aux_ref) in enumerate(((own_ref, own_aux_ref), (sib_ref, sib_aux_ref))):
        for i in range(rows // LANES):
            columns = slice(i * LANES, (i + 1) * LANES)
            inner = lax.dot_general(
                block, obs_ref[columns, :], (((1,), (1,)), ((), ())), preferred_element_type=jnp.float32
            )
            scale = aux_ref[0:1, columns]
            active = sim_class == aux_ref[step + 1 : step + 2, columns]
            score = jnp.where(active, inner - half_square, -jnp.inf)
            old = state_ref[half, 0:1, columns]
            top = jnp.maximum(old, jnp.max(score, axis=0, keepdims=True))
            factor = jnp.exp2((old - top) * scale)
            weights = jnp.exp2((score - top) * scale)
            total = state_ref[half, 1:2, columns] * factor + jnp.sum(weights, axis=0, keepdims=True)
            added = lax.dot_general(
                params, weights.astype(jnp.bfloat16), (((1,), (0,)), ((), ())), preferred_element_type=jnp.float32
            )
            out_ref[half, 0:1, columns] = top
            out_ref[half, 1:2, columns] = total
            out_ref[half, 2:6, columns] = state_ref[half, 2:6, columns] * factor + added[0:4]
            out_ref[half, 6:8, columns] = state_ref[half, 6:8, columns]


def finish_kernel(size, mine_ref, other_ref, aux_ref, square_ref, mean_ref, evidence_ref):
    scale = aux_ref[0:1, :]
    top_a, top_b = mine_ref[0:1, :], other_ref[0:1, :]
    top = jnp.maximum(top_a, top_b)
    factor_a = jnp.exp2((top_a - top) * scale)
    factor_b = jnp.exp2((top_b - top) * scale)
    total = mine_ref[1:2, :] * factor_a + other_ref[1:2, :] * factor_b
    sums = mine_ref[2:6, :] * factor_a + other_ref[2:6, :] * factor_b
    mean_ref[...] = sums / total
    sharp = scale * (0.5 / LOG2E)
    evidence = sharp * (2.0 * size - square_ref[0:1, :] + 2.0 * top) + jnp.log(total)
    evidence_ref[...] = evidence.reshape(evidence_ref.shape)


def on_device(pairs, order, observed, sharpness, obs_class, pattern, evolved, sim_params, sim_class):
    rows, size = observed.shape
    count = evolved.shape[0]
    steps = len(order[0])
    aux_rows = -(-(steps + 1) // SUBLANES) * SUBLANES
    vmem = pl.BlockSpec(memory_space=pltpu.VMEM)
    smem = pl.BlockSpec(memory_space=pltpu.SMEM)
    params = pltpu.CompilerParams(vmem_limit_bytes=VMEM_LIMIT)
    f32 = jnp.float32
    core = [(i, i ^ 1) for i in range(len(order))]

    observed_sib = lax.ppermute(observed, "blk", core)
    own_aux, sib_aux, meta, square = pl.pallas_call(
        prepare_kernel,
        out_shape=(
            jax.ShapeDtypeStruct((aux_rows, rows), f32),
            jax.ShapeDtypeStruct((aux_rows, rows), f32),
            jax.ShapeDtypeStruct((SUBLANES, count), f32),
            jax.ShapeDtypeStruct((SUBLANES, rows), f32),
        ),
        in_specs=[smem, smem, smem, vmem, vmem, vmem, vmem, vmem],
        out_specs=(vmem,) * 4,
        compiler_params=params,
        name="prepare",
    )(
        lax.axis_index("blk").reshape(1), jnp.array(order, jnp.int32), pattern, obs_class, sharpness, observed,
        sim_params, sim_class,
    )
    sib_aux = lax.ppermute(sib_aux, "blk", core)

    state = jnp.zeros((2, SUBLANES, rows), f32).at[:, 0].set(NEG_START)

    def absorb(step, block, about, state):
        return pl.pallas_call(
            functools.partial(absorb_kernel, step),
            out_shape=jax.ShapeDtypeStruct(state.shape, f32),
            in_specs=[vmem] * 7,
            out_specs=vmem,
            compiler_params=params,
            cost_estimate=pl.CostEstimate(
                flops=4 * rows * count * size, bytes_accessed=4 * rows * size, transcendentals=2 * rows * count
            ),
            name="absorb",
        )(observed, observed_sib, own_aux, sib_aux, block, about, state)

    held = [(evolved, meta), (evolved, meta)]
    state = absorb(0, evolved, meta, state)
    for step in range(steps - 1):
        kind = step % 2
        held[kind] = tuple(lax.ppermute(part, "blk", pairs[kind]) for part in held[kind])
        state = absorb(step + 1, *held[kind], state)

    other = lax.ppermute(state[1], "blk", core)
    mean, evidence = pl.pallas_call(
        functools.partial(finish_kernel, size),
        out_shape=(jax.ShapeDtypeStruct((sim_params.shape[0], rows), f32), jax.ShapeDtypeStruct((rows,), f32)),
        in_specs=[vmem] * 4,
        out_specs=(vmem,) * 2,
        compiler_params=params,
        name="finish",
    )(state[0], other, own_aux, square)
    return mean, evidence


def solution(mesh):
    placed = (
        P(("parts", "blk"), None),
        P(("parts", "blk")),
        P(("parts", "blk")),
        P(("parts", "blk"), None),
        P(("parts", "blk"), None),
        P(None, ("parts", "blk")),
        P(("parts", "blk")),
    )
    pairs, order = plan(mesh.shape["blk"], mesh.shape["parts"] == 2)
    return jax.shard_map(
        functools.partial(on_device, pairs, order),
        mesh=mesh,
        in_specs=placed,
        out_specs=(P(None, ("parts", "blk")), P(("parts", "blk"))),
        check_vma=False,
    )
```

```python
import functools
import math

import jax
import jax.numpy as jnp
import numpy as np
from jax import lax
from jax.experimental import pallas as pl
from jax.experimental.pallas import tpu as pltpu
from jax.sharding import PartitionSpec as P

NEG_START = -1e30
LOG2E = math.log2(math.e)
SUBLANES = 8
VMEM_LIMIT = 40 * 1024 * 1024


def plan(size, grid):
    chips = size // 2

    def ring(place):
        if not grid:
            return place
        return jnp.where(place < chips // 2, 2 * place, 2 * (chips - 1 - place) + 1)

    def place_of(chip):
        if not grid:
            return chip
        return jnp.where(chip % 2 == 0, chip // 2, chips - 1 - chip // 2)

    def beside(device, by):
        return ring((place_of(device // 2) + by + chips) % chips) * 2 + device % 2

    def way(device, kind):
        return 1 - 2 * ((device + kind) % 2)

    def block_of(device, step):
        if step == 0:
            return device
        return beside(device, -way(device, (step - 1) % 2) * ((step + 1) // 2))

    all_devices = np.arange(size)
    with jax.ensure_compile_time_eval():
        targets = [np.asarray(beside(all_devices, way(all_devices, kind))).tolist() for kind in range(2)]
    return [list(enumerate(target)) for target in targets], block_of


def joined(parts, axis):
    return parts[0] if len(parts) == 1 else jnp.concatenate(parts, axis=axis)


def lanes_of(aux_ref, at):
    return jnp.concatenate([aux_ref[i, pl.ds(at, 1), :] for i in range(aux_ref.shape[0])], axis=1)


def norms(observed):
    wide = observed.astype(jnp.float32)
    square = wide * wide
    high = square.astype(jnp.bfloat16)
    low = (square - high.astype(jnp.float32)).astype(jnp.bfloat16)
    ones = jnp.ones((SUBLANES, observed.shape[1]), jnp.bfloat16)
    return sum(
        lax.dot_general(ones, part, (((1,), (1,)), ((), ())), preferred_element_type=jnp.float32)[0:1]
        for part in (high, low)
    )


def absorb_kernel(steps, block_of, half, first, at_ref, observed_ref, aux_ref, *refs):
    count = len(steps)
    block_refs, meta_refs, out_ref = refs[:count], refs[count : 2 * count], refs[-1]
    inner = lax.dot_general(
        joined([ref[...] for ref in block_refs], 0), observed_ref[...],
        (((1,), (1,)), ((), ())), preferred_element_type=jnp.float32,
    )
    scale = lanes_of(aux_ref, aux_ref.shape[1] - 1) * (2.0 * LOG2E)
    metas = [ref[...] for ref in meta_refs]
    if first:
        top = jnp.full(scale.shape, NEG_START, jnp.float32)
    else:
        state_ref = refs[2 * count]
        top = old = state_ref[0:1, :]
    scores = []
    for i, (step, block_ref, meta) in enumerate(zip(steps, block_refs, metas)):
        rows = block_ref.shape[0]
        wide = block_ref[...].astype(jnp.float32)
        half_square = 0.5 * jnp.sum(wide * wide, axis=1, keepdims=True)
        padded = jnp.concatenate([meta] + [jnp.zeros_like(meta)] * (rows // SUBLANES - 1), axis=0)
        active = padded.T[:, SUBLANES - 1 : SUBLANES] == lanes_of(aux_ref, block_of(at_ref[0], step))
        score = jnp.where(active, inner[i * rows : (i + 1) * rows] - half_square, -jnp.inf)
        top = jnp.maximum(top, jnp.max(score, axis=0, keepdims=True))
        scores.append(score)
    weights = [jnp.exp2((score - top) * scale) for score in scores]
    total = sum(jnp.sum(weight, axis=0, keepdims=True) for weight in weights)
    sums = lax.dot_general(
        joined([meta.astype(jnp.bfloat16) for meta in metas], 1),
        joined([weight.astype(jnp.bfloat16) for weight in weights], 0),
        (((1,), (0,)), ((), ())), preferred_element_type=jnp.float32,
    )[0:4]
    if not first:
        factor = jnp.exp2((old - top) * scale)
        total += state_ref[1:2, :] * factor
        sums += state_ref[2:6, :] * factor
    out_ref[0:1, :] = top
    out_ref[1:2, :] = total
    out_ref[2:6, :] = sums
    if half == 1:
        out_ref[6:8, :] = jnp.zeros_like(out_ref[6:8, :])
    elif first:
        out_ref[6:8, :] = jnp.broadcast_to(norms(observed_ref[...]), out_ref[6:8, :].shape)
    else:
        out_ref[6:8, :] = state_ref[6:8, :]


def finish_kernel(size, mine_ref, other_ref, aux_ref, mean_ref, evidence_ref):
    sharp = lanes_of(aux_ref, aux_ref.shape[1] - 1)
    scale = sharp * (2.0 * LOG2E)
    top_a, top_b = mine_ref[0:1, :], other_ref[0:1, :]
    top = jnp.maximum(top_a, top_b)
    factor_a = jnp.exp2((top_a - top) * scale)
    factor_b = jnp.exp2((top_b - top) * scale)
    total = mine_ref[1:2, :] * factor_a + other_ref[1:2, :] * factor_b
    sums = mine_ref[2:6, :] * factor_a + other_ref[2:6, :] * factor_b
    mean_ref[...] = sums / total
    evidence = sharp * (2.0 * size - mine_ref[6:7, :] + 2.0 * top) + jnp.log(total)
    evidence_ref[...] = evidence.reshape(evidence_ref.shape)


def after(values, *earlier):
    return lax.optimization_barrier((values, earlier))[0]


def on_device(pairs, block_of, observed, sharpness, obs_class, pattern, evolved, sim_params, sim_class):
    rows, size = observed.shape
    count = evolved.shape[0]
    tiles, devices = pattern.shape
    steps = devices // 2
    tile = rows // tiles
    vmem = pl.BlockSpec(memory_space=pltpu.VMEM)
    smem = pl.BlockSpec(memory_space=pltpu.SMEM)
    compiler_params = pltpu.CompilerParams(vmem_limit_bytes=VMEM_LIMIT)
    f32 = jnp.float32
    core = [(i, i ^ 1) for i in range(devices)]
    at = lax.axis_index("blk").astype(jnp.int32).reshape(1)

    blocks = [evolved]
    moving = [evolved, evolved]

    def send(step):
        kind = step % 2
        moving[kind] = lax.ppermute(moving[kind], "blk", pairs[kind])
        blocks.append(moving[kind])

    send(0)
    observed_sib = lax.ppermute(observed, "blk", core)
    classes = obs_class.astype(f32).reshape(tiles, 1, tile)
    own_aux = jnp.concatenate(
        [
            jnp.where(pattern[:, :, None] == 1, classes, -1.0),
            jnp.broadcast_to(sharpness.reshape(tiles, 1, tile), (tiles, SUBLANES, tile)),
        ],
        axis=1,
    )
    meta = jnp.concatenate(
        [
            sim_params.astype(f32),
            jnp.broadcast_to(sim_class.astype(f32)[None, :], (SUBLANES - sim_params.shape[0], count)),
        ],
        axis=0,
    )
    sib_aux = lax.ppermute(own_aux, "blk", core)
    metas = [meta]
    moving_meta = [meta, meta]

    def absorb(work, half, state):
        observed_half, aux = ((observed, own_aux), (observed_sib, sib_aux))[half]
        before = () if state is None else (state,)
        return pl.pallas_call(
            functools.partial(absorb_kernel, work, block_of, half, state is None),
            out_shape=jax.ShapeDtypeStruct((SUBLANES, rows), f32),
            in_specs=[smem] + [vmem] * (2 + 2 * len(work) + len(before)),
            out_specs=vmem,
            compiler_params=compiler_params,
            cost_estimate=pl.CostEstimate(
                flops=2 * len(work) * rows * count * size,
                bytes_accessed=2 * (rows + len(work) * count) * size,
                transcendentals=len(work) * rows * count,
            ),
            name="absorb",
        )(at, observed_half, aux, *(blocks[i] for i in work), *(metas[i] for i in work), *before)

    def send_meta(step):
        kind = step % 2
        moving_meta[kind] = lax.ppermute(moving_meta[kind], "blk", pairs[kind])
        metas.append(moving_meta[kind])

    send_meta(0)
    moving[1] = after(moving[1], meta, own_aux)
    send(1)
    send_meta(1)
    states = [None, None]
    works = []
    for first in range(0, steps, 2):
        work = tuple(range(first, min(first + 2, steps)))
        works += [(work, half) for half in ((0, 1) if first + 2 < steps else (1, 0))]
    done = []
    for step in range(steps - 1):
        ahead = step + 2
        if ahead < steps - 1:
            kind = ahead % 2
            if done:
                moving[kind], moving_meta[kind] = after((moving[kind], moving_meta[kind]), done[-1])
            send(ahead)
            send_meta(ahead)
        if step < len(works):
            work, half = works[step]
            states[half] = absorb(work, half, states[half])
            done.append(states[half])
    for work, half in works[steps - 1 : -1]:
        states[half] = absorb(work, half, states[half])
    other = lax.ppermute(states[1], "blk", core)
    work, half = works[-1]
    states[half] = absorb(work, half, states[half])
    mean, evidence = pl.pallas_call(
        functools.partial(finish_kernel, size),
        out_shape=(jax.ShapeDtypeStruct((sim_params.shape[0], rows), f32), jax.ShapeDtypeStruct((rows,), f32)),
        in_specs=[vmem] * 3,
        out_specs=(vmem,) * 2,
        compiler_params=compiler_params,
        name="finish",
    )(states[0], other, own_aux)
    return mean, evidence


def solution(mesh):
    placed = (
        P(("parts", "blk"), None),
        P(("parts", "blk")),
        P(("parts", "blk")),
        P(("parts", "blk"), None),
        P(("parts", "blk"), None),
        P(None, ("parts", "blk")),
        P(("parts", "blk")),
    )
    pairs, block_of = plan(mesh.shape["blk"], mesh.shape["parts"] == 2)
    return jax.shard_map(
        functools.partial(on_device, pairs, block_of),
        mesh=mesh,
        in_specs=placed,
        out_specs=(P(None, ("parts", "blk")), P(("parts", "blk"))),
        check_vma=False,
    )
```

```python
import functools
import math

import jax
import jax.numpy as jnp
import numpy as np
from jax import lax
from jax.experimental import pallas as pl
from jax.experimental.pallas import tpu as pltpu
from jax.sharding import PartitionSpec as P

NEG_START = -1e30
LOG2E = math.log2(math.e)
SUBLANES = 8
LANES = 128
META_ROWS = 16
VMEM_LIMIT = 40 * 1024 * 1024


def plan(size, grid):
    chips = size // 2

    def ring(place):
        if not grid:
            return place
        return jnp.where(place < chips // 2, 2 * place, 2 * (chips - 1 - place) + 1)

    def place_of(chip):
        if not grid:
            return chip
        return jnp.where(chip % 2 == 0, chip // 2, chips - 1 - chip // 2)

    def beside(device, by):
        return ring((place_of(device // 2) + by + chips) % chips) * 2 + device % 2

    def way(device, kind):
        return 1 - 2 * ((device + kind) % 2)

    def block_of(device, step):
        if step == 0:
            return device
        return beside(device, -way(device, (step - 1) % 2) * ((step + 1) // 2))

    all_devices = np.arange(size)
    with jax.ensure_compile_time_eval():
        targets = [np.asarray(beside(all_devices, way(all_devices, kind))).tolist() for kind in range(2)]
    return [list(enumerate(target)) for target in targets], block_of


def joined(parts, axis):
    return parts[0] if len(parts) == 1 else jnp.concatenate(parts, axis=axis)


def row(values):
    return values.reshape(1, values.shape[-1])


def pack_kernel(params_hbm, class_hbm, evolved_hbm, packet_ref, params_ref, class_ref, arrived):
    rows, size = evolved_hbm.shape
    panels = size // LANES
    copies = [
        pltpu.make_async_copy(params_hbm, params_ref, arrived.at[0]),
        pltpu.make_async_copy(class_hbm, class_ref, arrived.at[1]),
    ]
    for i in range(panels):
        panel = packet_ref.at[pl.ds(i * rows, rows), :]
        source = evolved_hbm.at[:, pl.ds(i * LANES, LANES)]
        copies.append(pltpu.make_async_copy(source, panel, arrived.at[i + 2]))
    for copy in copies:
        copy.start()
    for copy in copies[:2]:
        copy.wait()
    params = params_ref[...].astype(jnp.float32)
    classes = row(class_ref[...]).astype(jnp.float32)
    rest = jnp.broadcast_to(classes, (META_ROWS - params.shape[0], classes.shape[1]))
    packet_ref[panels * rows :, :] = jnp.concatenate([params, rest], axis=0).astype(packet_ref.dtype)
    for copy in copies[2:]:
        copy.wait()


def norms(observed):
    wide = observed.astype(jnp.float32)
    square = wide * wide
    high = square.astype(jnp.bfloat16)
    low = (square - high.astype(jnp.float32)).astype(jnp.bfloat16)
    ones = jnp.ones((SUBLANES, observed.shape[1]), jnp.bfloat16)
    return sum(
        lax.dot_general(ones, part, (((1,), (1,)), ((), ())), preferred_element_type=jnp.float32)[0:1]
        for part in (high, low)
    )


def prepare_kernel(
    block_of, at_ref, pattern_hbm, class_hbm, sharp_hbm, observed_hbm,
    own_ref, sib_ref, observed_ref, pattern_ref, class_ref, sharp_ref, arrived,
):
    sources = (pattern_hbm, class_hbm, sharp_hbm, observed_hbm)
    targets = (pattern_ref, class_ref, sharp_ref, observed_ref)
    copies = [
        pltpu.make_async_copy(source, target, arrived.at[i])
        for i, (source, target) in enumerate(zip(sources, targets))
    ]
    for copy in copies:
        copy.start()
    for copy in copies[:3]:
        copy.wait()
    tiles, devices = pattern_ref.shape
    tile = class_ref.shape[0] // tiles
    classes = row(class_ref[...]).astype(jnp.float32)
    scale = row(sharp_ref[...]) * (2.0 * LOG2E)
    for out_ref, device in ((own_ref, at_ref[0]), (sib_ref, at_ref[0] ^ 1)):
        for step in range(devices // 2):
            block = block_of(device, step)
            opened = [
                jnp.where(pattern_ref[i, block] == 1, classes[:, i * tile : (i + 1) * tile], -1.0) for i in range(tiles)
            ]
            out_ref[step : step + 1, :] = jnp.concatenate(opened, axis=1)
        out_ref[devices // 2 : devices // 2 + 1, :] = scale
    copies[3].wait()
    own_ref[devices // 2 + 1 : devices // 2 + 2, :] = norms(observed_ref[...])
    sib_ref[devices // 2 + 1 : devices // 2 + 2, :] = scale


def absorb_kernel(steps, count, first, observed_ref, aux_ref, *refs):
    packet_refs, out_ref = refs[: len(steps)], refs[-1]
    panels = observed_ref.shape[1] // LANES
    blocks = [jnp.concatenate([ref[i * count : (i + 1) * count, :] for i in range(panels)], axis=1) for ref in packet_refs]
    inner = lax.dot_general(
        joined(blocks, 0), observed_ref[...], (((1,), (1,)), ((), ())), preferred_element_type=jnp.float32
    )
    metas = [ref[panels * count :, :] for ref in packet_refs]
    after_steps = aux_ref.shape[0] - 2
    scale = aux_ref[after_steps : after_steps + 1, :]
    if first:
        top = jnp.full(scale.shape, NEG_START, jnp.float32)
    else:
        state_ref = refs[len(steps)]
        top = old = state_ref[0:1, :]
    scores = []
    for i, (step, block, meta) in enumerate(zip(steps, blocks, metas)):
        wide = block.astype(jnp.float32)
        half_square = 0.5 * jnp.sum(wide * wide, axis=1, keepdims=True)
        classes = meta[META_ROWS // 2 :].astype(jnp.float32)
        column = jnp.concatenate([classes] * (count // SUBLANES), axis=0).T[:, 0:1]
        active = column == aux_ref[step : step + 1, :]
        score = jnp.where(active, inner[i * count : (i + 1) * count] - half_square, -jnp.inf)
        top = jnp.maximum(top, jnp.max(score, axis=0, keepdims=True))
        scores.append(score)
    weights = [jnp.exp2((score - top) * scale) for score in scores]
    total = sum(jnp.sum(weight, axis=0, keepdims=True) for weight in weights)
    sums = lax.dot_general(
        joined(metas, 1), joined([weight.astype(jnp.bfloat16) for weight in weights], 0),
        (((1,), (0,)), ((), ())), preferred_element_type=jnp.float32,
    )[0:4]
    if not first:
        factor = jnp.exp2((old - top) * scale)
        total += state_ref[1:2, :] * factor
        sums += state_ref[2:6, :] * factor
    out_ref[0:1, :] = top
    out_ref[1:2, :] = total
    out_ref[2:6, :] = sums
    out_ref[6:8, :] = jnp.zeros_like(out_ref[6:8, :])


def finish_kernel(size, mine_ref, other_ref, aux_ref, mean_ref, evidence_ref):
    after_steps = aux_ref.shape[0] - 2
    scale = aux_ref[after_steps : after_steps + 1, :]
    top_a, top_b = mine_ref[0:1, :], other_ref[0:1, :]
    top = jnp.maximum(top_a, top_b)
    factor_a = jnp.exp2((top_a - top) * scale)
    factor_b = jnp.exp2((top_b - top) * scale)
    total = mine_ref[1:2, :] * factor_a + other_ref[1:2, :] * factor_b
    sums = mine_ref[2:6, :] * factor_a + other_ref[2:6, :] * factor_b
    mean_ref[...] = sums / total
    sharp = scale * (0.5 / LOG2E)
    evidence = sharp * (2.0 * size - aux_ref[after_steps + 1 : after_steps + 2, :] + 2.0 * top) + jnp.log(total)
    evidence_ref[...] = evidence.reshape(evidence_ref.shape)


def after(values, *earlier):
    return lax.optimization_barrier((values, earlier))[0]


def in_hbm(*arrays):
    return [pltpu.with_memory_space_constraint(array, pltpu.HBM) for array in arrays]


def on_device(pairs, block_of, observed, sharpness, obs_class, pattern, evolved, sim_params, sim_class):
    rows, size = observed.shape
    count = evolved.shape[0]
    devices = pattern.shape[1]
    steps = devices // 2
    vmem = pl.BlockSpec(memory_space=pltpu.VMEM)
    smem = pl.BlockSpec(memory_space=pltpu.SMEM)
    hbm = pl.BlockSpec(memory_space=pltpu.HBM)
    compiler_params = pltpu.CompilerParams(vmem_limit_bytes=VMEM_LIMIT)
    f32 = jnp.float32
    core = [(i, i ^ 1) for i in range(devices)]
    at = lax.axis_index("blk").astype(jnp.int32).reshape(1)

    packet = pl.pallas_call(
        pack_kernel,
        out_shape=jax.ShapeDtypeStruct((count * size // LANES + META_ROWS, LANES), evolved.dtype),
        in_specs=[hbm] * 3,
        out_specs=vmem,
        scratch_shapes=[
            pltpu.VMEM(sim_params.shape, sim_params.dtype),
            pltpu.VMEM(sim_class.shape, sim_class.dtype),
            pltpu.SemaphoreType.DMA((size // LANES + 2,)),
        ],
        compiler_params=compiler_params,
        name="pack",
    )(*in_hbm(sim_params, sim_class, evolved))
    packets = [packet]
    moving = [packet, packet]

    def send(step):
        kind = step % 2
        moving[kind] = lax.ppermute(moving[kind], "blk", pairs[kind])
        packets.append(moving[kind])

    send(0)
    own_aux, sib_aux, observed_own = pl.pallas_call(
        functools.partial(prepare_kernel, block_of),
        out_shape=(
            jax.ShapeDtypeStruct((steps + 2, rows), f32),
            jax.ShapeDtypeStruct((steps + 2, rows), f32),
            jax.ShapeDtypeStruct(observed.shape, observed.dtype),
        ),
        in_specs=[smem] + [hbm] * 4,
        out_specs=(vmem,) * 3,
        scratch_shapes=[
            pltpu.SMEM(pattern.shape, pattern.dtype),
            pltpu.VMEM(obs_class.shape, obs_class.dtype),
            pltpu.VMEM(sharpness.shape, sharpness.dtype),
            pltpu.SemaphoreType.DMA((4,)),
        ],
        compiler_params=compiler_params,
        cost_estimate=pl.CostEstimate(flops=8 * rows * size, bytes_accessed=4 * rows * size, transcendentals=0),
        name="prepare",
    )(after(at, packet), *in_hbm(pattern, obs_class, sharpness, observed))
    observed_sib = lax.ppermute(observed, "blk", core)
    sib_aux = lax.ppermute(sib_aux, "blk", core)
    moving[1] = after(moving[1], own_aux)
    send(1)

    def absorb(work, half, state):
        observed_half, aux = ((observed_own, own_aux), (observed_sib, sib_aux))[half]
        before = () if state is None else (state,)
        return pl.pallas_call(
            functools.partial(absorb_kernel, work, count, state is None),
            out_shape=jax.ShapeDtypeStruct((SUBLANES, rows), f32),
            in_specs=[vmem] * (2 + len(work) + len(before)),
            out_specs=vmem,
            compiler_params=compiler_params,
            cost_estimate=pl.CostEstimate(
                flops=2 * len(work) * rows * count * size,
                bytes_accessed=2 * (rows + len(work) * count) * size,
                transcendentals=len(work) * rows * count,
            ),
            name="absorb",
        )(observed_half, aux, *(packets[i] for i in work), *before)

    states = [None, None]
    works = []
    for first in range(0, steps, 2):
        work = tuple(range(first, min(first + 2, steps)))
        works += [(work, half) for half in ((0, 1) if first + 2 < steps else (1, 0))]
    done = []
    for step in range(steps - 1):
        ahead = step + 2
        if ahead < steps - 1:
            if done:
                moving[ahead % 2] = after(moving[ahead % 2], done[-1])
            send(ahead)
        if step < len(works):
            work, half = works[step]
            states[half] = absorb(work, half, states[half])
            done.append(states[half])
    for work, half in works[steps - 1 : -1]:
        states[half] = absorb(work, half, states[half])
    other = lax.ppermute(states[1], "blk", core)
    work, half = works[-1]
    states[half] = absorb(work, half, states[half])
    mean, evidence = pl.pallas_call(
        functools.partial(finish_kernel, size),
        out_shape=(jax.ShapeDtypeStruct((sim_params.shape[0], rows), f32), jax.ShapeDtypeStruct((rows,), f32)),
        in_specs=[vmem] * 3,
        out_specs=(vmem,) * 2,
        compiler_params=compiler_params,
        name="finish",
    )(states[0], other, own_aux)
    return mean, evidence


def solution(mesh):
    placed = (
        P(("parts", "blk"), None),
        P(("parts", "blk")),
        P(("parts", "blk")),
        P(("parts", "blk"), None),
        P(("parts", "blk"), None),
        P(None, ("parts", "blk")),
        P(("parts", "blk")),
    )
    pairs, block_of = plan(mesh.shape["blk"], mesh.shape["parts"] == 2)
    return jax.shard_map(
        functools.partial(on_device, pairs, block_of),
        mesh=mesh,
        in_specs=placed,
        out_specs=(P(None, ("parts", "blk")), P(("parts", "blk"))),
        check_vma=False,
    )
```

```python
import functools
import math

import jax
import jax.numpy as jnp
import numpy as np
from jax import lax
from jax.experimental import pallas as pl
from jax.experimental.pallas import tpu as pltpu
from jax.sharding import PartitionSpec as P

NEG_START = -1e30
LOG2E = math.log2(math.e)
SUBLANES = 8
LANES = 128
META_ROWS = 16
VMEM_LIMIT = 40 * 1024 * 1024


def plan(size, grid):
    chips = size // 2

    def ring(place):
        if not grid:
            return place
        return jnp.where(place < chips // 2, 2 * place, 2 * (chips - 1 - place) + 1)

    def place_of(chip):
        if not grid:
            return chip
        return jnp.where(chip % 2 == 0, chip // 2, chips - 1 - chip // 2)

    def beside(device, by):
        return ring((place_of(device // 2) + by + chips) % chips) * 2 + device % 2

    def block_of(device, step):
        return beside(device, step // 2 if step % 2 == 0 else -(step + 1) // 2)

    all_devices = np.arange(size)
    with jax.ensure_compile_time_eval():
        targets = [np.asarray(beside(all_devices, way)).tolist() for way in (1, -1, 1 - 2 * (all_devices % 2))]
    return [list(enumerate(target)) for target in targets], block_of


def joined(parts, axis):
    return parts[0] if len(parts) == 1 else jnp.concatenate(parts, axis=axis)


def row(values):
    return values.reshape(1, values.shape[-1])


def pack_kernel(params_hbm, class_hbm, evolved_hbm, observed_hbm, packet_ref, observed_ref, params_ref, class_ref, arrived):
    rows, size = evolved_hbm.shape
    panels = size // LANES
    copies = [
        pltpu.make_async_copy(params_hbm, params_ref, arrived.at[0]),
        pltpu.make_async_copy(class_hbm, class_ref, arrived.at[1]),
    ]
    for i in range(panels):
        panel = packet_ref.at[pl.ds(i * rows, rows), :]
        source = evolved_hbm.at[:, pl.ds(i * LANES, LANES)]
        copies.append(pltpu.make_async_copy(source, panel, arrived.at[i + 2]))
    copies.append(pltpu.make_async_copy(observed_hbm, observed_ref, arrived.at[panels + 2]))
    for copy in copies:
        copy.start()
    for copy in copies[:2]:
        copy.wait()
    params = params_ref[...].astype(jnp.float32)
    classes = row(class_ref[...]).astype(jnp.float32)
    rest = jnp.broadcast_to(classes, (META_ROWS - params.shape[0], classes.shape[1]))
    packet_ref[panels * rows :, :] = jnp.concatenate([params, rest], axis=0).astype(packet_ref.dtype)
    for copy in copies[2:]:
        copy.wait()


def norms(observed):
    wide = observed.astype(jnp.float32)
    square = wide * wide
    high = square.astype(jnp.bfloat16)
    low = (square - high.astype(jnp.float32)).astype(jnp.bfloat16)
    ones = jnp.ones((SUBLANES, observed.shape[1]), jnp.bfloat16)
    return sum(
        lax.dot_general(ones, part, (((1,), (1,)), ((), ())), preferred_element_type=jnp.float32)[0:1]
        for part in (high, low)
    )


def prepare_kernel(
    block_of, at_ref, pattern_hbm, class_hbm, sharp_hbm, observed_ref,
    own_ref, sib_ref, pattern_ref, class_ref, sharp_ref, arrived,
):
    sources = (pattern_hbm, class_hbm, sharp_hbm)
    targets = (pattern_ref, class_ref, sharp_ref)
    copies = [
        pltpu.make_async_copy(source, target, arrived.at[i])
        for i, (source, target) in enumerate(zip(sources, targets))
    ]
    for copy in copies:
        copy.start()
    after_steps = own_ref.shape[0] - 2
    own_ref[after_steps + 1 : after_steps + 2, :] = norms(observed_ref[...])
    for copy in copies:
        copy.wait()
    tiles, devices = pattern_ref.shape
    tile = class_ref.shape[0] // tiles
    classes = row(class_ref[...]).astype(jnp.float32)
    scale = row(sharp_ref[...]) * (2.0 * LOG2E)
    for out_ref, device in ((own_ref, at_ref[0]), (sib_ref, at_ref[0] ^ 1)):
        for step in range(devices // 2):
            block = block_of(device, step)
            opened = [
                jnp.where(pattern_ref[i, block] == 1, classes[:, i * tile : (i + 1) * tile], -1.0) for i in range(tiles)
            ]
            out_ref[step : step + 1, :] = jnp.concatenate(opened, axis=1)
        out_ref[after_steps : after_steps + 1, :] = scale
    sib_ref[after_steps + 1 : after_steps + 2, :] = scale


def choose_kernel(at_ref, first_ref, second_ref, out_ref):
    core = at_ref[0] % 2

    @pl.when(core == 0)
    def _():
        out_ref[...] = first_ref[...]

    @pl.when(core == 1)
    def _():
        out_ref[...] = second_ref[...]


def absorb_kernel(steps, count, first, observed_ref, aux_ref, *refs):
    packet_refs, out_ref = refs[: len(steps)], refs[-1]
    panels = observed_ref.shape[1] // LANES
    blocks = [jnp.concatenate([ref[i * count : (i + 1) * count, :] for i in range(panels)], axis=1) for ref in packet_refs]
    inner = lax.dot_general(
        joined(blocks, 0), observed_ref[...], (((1,), (1,)), ((), ())), preferred_element_type=jnp.float32
    )
    metas = [ref[panels * count :, :] for ref in packet_refs]
    after_steps = aux_ref.shape[0] - 2
    scale = aux_ref[after_steps : after_steps + 1, :]
    if first:
        top = jnp.full(scale.shape, NEG_START, jnp.float32)
    else:
        state_ref = refs[len(steps)]
        top = old = state_ref[0:1, :]
    scores = []
    for i, (step, block, meta) in enumerate(zip(steps, blocks, metas)):
        wide = block.astype(jnp.float32)
        half_square = 0.5 * jnp.sum(wide * wide, axis=1, keepdims=True)
        classes = meta[META_ROWS // 2 :].astype(jnp.float32)
        column = jnp.concatenate([classes] * (count // SUBLANES), axis=0).T[:, 0:1]
        active = column == aux_ref[step : step + 1, :]
        score = jnp.where(active, inner[i * count : (i + 1) * count] - half_square, -jnp.inf)
        top = jnp.maximum(top, jnp.max(score, axis=0, keepdims=True))
        scores.append(score)
    weights = [jnp.exp2((score - top) * scale) for score in scores]
    total = sum(jnp.sum(weight, axis=0, keepdims=True) for weight in weights)
    sums = lax.dot_general(
        joined(metas, 1), joined([weight.astype(jnp.bfloat16) for weight in weights], 0),
        (((1,), (0,)), ((), ())), preferred_element_type=jnp.float32,
    )[0:4]
    if not first:
        factor = jnp.exp2((old - top) * scale)
        total += state_ref[1:2, :] * factor
        sums += state_ref[2:6, :] * factor
    out_ref[0:1, :] = top
    out_ref[1:2, :] = total
    out_ref[2:6, :] = sums
    out_ref[6:8, :] = jnp.zeros_like(out_ref[6:8, :])


def finish_kernel(size, mine_ref, other_ref, aux_ref, mean_ref, evidence_ref):
    after_steps = aux_ref.shape[0] - 2
    scale = aux_ref[after_steps : after_steps + 1, :]
    top_a, top_b = mine_ref[0:1, :], other_ref[0:1, :]
    top = jnp.maximum(top_a, top_b)
    factor_a = jnp.exp2((top_a - top) * scale)
    factor_b = jnp.exp2((top_b - top) * scale)
    total = mine_ref[1:2, :] * factor_a + other_ref[1:2, :] * factor_b
    sums = mine_ref[2:6, :] * factor_a + other_ref[2:6, :] * factor_b
    mean_ref[...] = sums / total
    sharp = scale * (0.5 / LOG2E)
    evidence = sharp * (2.0 * size - aux_ref[after_steps + 1 : after_steps + 2, :] + 2.0 * top) + jnp.log(total)
    evidence_ref[...] = evidence.reshape(evidence_ref.shape)


def after(values, *earlier):
    return lax.optimization_barrier((values, earlier))[0]


def in_hbm(*arrays):
    return [pltpu.with_memory_space_constraint(array, pltpu.HBM) for array in arrays]


def on_device(pairs, block_of, observed, sharpness, obs_class, pattern, evolved, sim_params, sim_class):
    rows, size = observed.shape
    count = evolved.shape[0]
    devices = pattern.shape[1]
    steps = devices // 2
    vmem = pl.BlockSpec(memory_space=pltpu.VMEM)
    smem = pl.BlockSpec(memory_space=pltpu.SMEM)
    hbm = pl.BlockSpec(memory_space=pltpu.HBM)
    compiler_params = pltpu.CompilerParams(vmem_limit_bytes=VMEM_LIMIT)
    f32 = jnp.float32
    core = [(i, i ^ 1) for i in range(devices)]
    at = lax.axis_index("blk").astype(jnp.int32).reshape(1)

    packet, observed_own = pl.pallas_call(
        pack_kernel,
        out_shape=(
            jax.ShapeDtypeStruct((count * size // LANES + META_ROWS, LANES), evolved.dtype),
            jax.ShapeDtypeStruct(observed.shape, observed.dtype),
        ),
        in_specs=[hbm] * 4,
        out_specs=(vmem,) * 2,
        scratch_shapes=[
            pltpu.VMEM(sim_params.shape, sim_params.dtype),
            pltpu.VMEM(sim_class.shape, sim_class.dtype),
            pltpu.SemaphoreType.DMA((size // LANES + 3,)),
        ],
        compiler_params=compiler_params,
        name="pack",
    )(*in_hbm(sim_params, sim_class, evolved, observed))
    forward = lax.ppermute(packet, "blk", pairs[0])
    backward = lax.ppermute(packet, "blk", pairs[1])
    observed_sib = lax.ppermute(observed_own, "blk", core)
    own_aux, sib_aux = pl.pallas_call(
        functools.partial(prepare_kernel, block_of),
        out_shape=(
            jax.ShapeDtypeStruct((steps + 2, rows), f32),
            jax.ShapeDtypeStruct((steps + 2, rows), f32),
        ),
        in_specs=[smem] + [hbm] * 3 + [vmem],
        out_specs=(vmem,) * 2,
        scratch_shapes=[
            pltpu.SMEM(pattern.shape, pattern.dtype),
            pltpu.VMEM(obs_class.shape, obs_class.dtype),
            pltpu.VMEM(sharpness.shape, sharpness.dtype),
            pltpu.SemaphoreType.DMA((3,)),
        ],
        compiler_params=compiler_params,
        cost_estimate=pl.CostEstimate(flops=8 * rows * size, bytes_accessed=4 * rows * size, transcendentals=0),
        name="prepare",
    )(at, *in_hbm(pattern, obs_class, sharpness), observed_own)
    sib_aux = lax.ppermute(sib_aux, "blk", core)
    packets = [packet]

    def absorb(work, half, state):
        observed_half, aux = ((observed_own, own_aux), (observed_sib, sib_aux))[half]
        before = () if state is None else (state,)
        return pl.pallas_call(
            functools.partial(absorb_kernel, work, count, state is None),
            out_shape=jax.ShapeDtypeStruct((SUBLANES, rows), f32),
            in_specs=[vmem] * (2 + len(work) + len(before)),
            out_specs=vmem,
            compiler_params=compiler_params,
            cost_estimate=pl.CostEstimate(
                flops=2 * len(work) * rows * count * size,
                bytes_accessed=2 * (rows + len(work) * count) * size,
                transcendentals=len(work) * rows * count,
            ),
            name="absorb",
        )(observed_half, aux, *(packets[i] for i in work), *before)

    states = [absorb((0,), 0, None), None]
    for step in range(1, steps - 1, 2):
        arrived = (forward, backward)
        packets += arrived
        last = step + 2 == steps - 1
        if last:
            chosen = pl.pallas_call(
                choose_kernel,
                out_shape=jax.ShapeDtypeStruct(packet.shape, packet.dtype),
                in_specs=[smem, vmem, vmem],
                out_specs=vmem,
                compiler_params=compiler_params,
                name="choose",
            )(at, *after(arrived, *(state for state in states if state is not None)))
            packets_last = lax.ppermute(chosen, "blk", pairs[2])
        else:
            before = [state for state in states if state is not None]
            forward = lax.ppermute(after(forward, *before), "blk", pairs[0])
            backward = lax.ppermute(after(backward, *before), "blk", pairs[1])
        states[0] = absorb((step, step + 1), 0, states[0])
        states[1] = absorb((step, step + 1) if states[1] is not None else (0, step, step + 1), 1, states[1])
    packets.append(after(packets_last, states[0]))
    states[1] = absorb((steps - 1,), 1, states[1])
    other = lax.ppermute(states[1], "blk", core)
    states[0] = absorb((steps - 1,), 0, states[0])
    mean, evidence = pl.pallas_call(
        functools.partial(finish_kernel, size),
        out_shape=(jax.ShapeDtypeStruct((sim_params.shape[0], rows), f32), jax.ShapeDtypeStruct((rows,), f32)),
        in_specs=[vmem] * 3,
        out_specs=(vmem,) * 2,
        compiler_params=compiler_params,
        name="finish",
    )(states[0], other, own_aux)
    return mean, evidence


def solution(mesh):
    placed = (
        P(("parts", "blk"), None),
        P(("parts", "blk")),
        P(("parts", "blk")),
        P(("parts", "blk"), None),
        P(("parts", "blk"), None),
        P(None, ("parts", "blk")),
        P(("parts", "blk")),
    )
    pairs, block_of = plan(mesh.shape["blk"], mesh.shape["parts"] == 2)
    return jax.shard_map(
        functools.partial(on_device, pairs, block_of),
        mesh=mesh,
        in_specs=placed,
        out_specs=(P(None, ("parts", "blk")), P(("parts", "blk"))),
        check_vma=False,
    )
```

```python
import functools
import math

import jax
import jax.numpy as jnp
import numpy as np
from jax import lax
from jax.experimental import pallas as pl
from jax.experimental.pallas import tpu as pltpu
from jax.sharding import PartitionSpec as P

NEG_START = -1e30
LOG2E = math.log2(math.e)
SUBLANES = 8
LANES = 128
META_ROWS = 16
VMEM_LIMIT = 40 * 1024 * 1024


def plan(size, grid):
    chips = size // 2

    def ring(place):
        if not grid:
            return place
        return jnp.where(place < chips // 2, 2 * place, 2 * (chips - 1 - place) + 1)

    def place_of(chip):
        if not grid:
            return chip
        return jnp.where(chip % 2 == 0, chip // 2, chips - 1 - chip // 2)

    def beside(device, by):
        return ring((place_of(device // 2) + by + chips) % chips) * 2 + (device + by) % 2

    def block_of(device, step):
        if step == 0:
            return device
        stream, hop = (step - 1) % 2, (step - 1) // 2
        way = 1 - 2 * ((device + 1 + stream + hop) % 2)
        return beside(device, -way * (hop + 1))

    devices = np.arange(size)
    with jax.ensure_compile_time_eval():
        targets = [np.asarray(beside(devices, 1 - 2 * ((devices + parity) % 2))).tolist() for parity in range(2)]
    return [list(enumerate(target)) for target in targets], block_of


def joined(parts, axis):
    return parts[0] if len(parts) == 1 else jnp.concatenate(parts, axis=axis)


def row(values):
    return values.reshape(1, values.shape[-1])


def pack_kernel(params_hbm, class_hbm, evolved_hbm, packet_ref, params_ref, class_ref, arrived):
    rows, size = evolved_hbm.shape
    panels = size // LANES
    copies = [
        pltpu.make_async_copy(params_hbm, params_ref, arrived.at[0]),
        pltpu.make_async_copy(class_hbm, class_ref, arrived.at[1]),
    ]
    for i in range(panels):
        panel = packet_ref.at[pl.ds(i * rows, rows), :]
        source = evolved_hbm.at[:, pl.ds(i * LANES, LANES)]
        copies.append(pltpu.make_async_copy(source, panel, arrived.at[i + 2]))
    for copy in copies:
        copy.start()
    for copy in copies[:2]:
        copy.wait()
    params = params_ref[...].astype(jnp.float32)
    classes = row(class_ref[...]).astype(jnp.float32)
    rest = jnp.broadcast_to(classes, (META_ROWS - params.shape[0], classes.shape[1]))
    packet_ref[panels * rows :, :] = jnp.concatenate([params, rest], axis=0).astype(packet_ref.dtype)
    for copy in copies[2:]:
        copy.wait()


def norms(observed):
    wide = observed.astype(jnp.float32)
    square = wide * wide
    high = square.astype(jnp.bfloat16)
    low = (square - high.astype(jnp.float32)).astype(jnp.bfloat16)
    ones = jnp.ones((SUBLANES, observed.shape[1]), jnp.bfloat16)
    return sum(
        lax.dot_general(ones, part, (((1,), (1,)), ((), ())), preferred_element_type=jnp.float32)[0:1]
        for part in (high, low)
    )


def prepare_kernel(
    block_of, at_ref, pattern_hbm, class_hbm, sharp_hbm, observed_hbm,
    own_ref, sib_ref, observed_ref, pattern_ref, class_ref, sharp_ref, arrived,
):
    sources = (pattern_hbm, class_hbm, sharp_hbm, observed_hbm)
    targets = (pattern_ref, class_ref, sharp_ref, observed_ref)
    copies = [
        pltpu.make_async_copy(source, target, arrived.at[i])
        for i, (source, target) in enumerate(zip(sources, targets))
    ]
    for copy in copies:
        copy.start()
    for copy in copies[:3]:
        copy.wait()
    tiles, devices = pattern_ref.shape
    tile = class_ref.shape[0] // tiles
    classes = row(class_ref[...]).astype(jnp.float32)
    scale = row(sharp_ref[...]) * (2.0 * LOG2E)
    for out_ref, device in ((own_ref, at_ref[0]), (sib_ref, at_ref[0] ^ 1)):
        for step in range(devices // 2):
            block = block_of(device, step)
            opened = [
                jnp.where(pattern_ref[i, block] == 1, classes[:, i * tile : (i + 1) * tile], -1.0) for i in range(tiles)
            ]
            out_ref[step : step + 1, :] = jnp.concatenate(opened, axis=1)
        out_ref[devices // 2 : devices // 2 + 1, :] = scale
    copies[3].wait()
    own_ref[devices // 2 + 1 : devices // 2 + 2, :] = norms(observed_ref[...])
    sib_ref[devices // 2 + 1 : devices // 2 + 2, :] = scale


def absorb_kernel(steps, count, first, observed_ref, aux_ref, *refs):
    packet_refs, out_ref = refs[: len(steps)], refs[-1]
    panels = observed_ref.shape[1] // LANES
    blocks = [jnp.concatenate([ref[i * count : (i + 1) * count, :] for i in range(panels)], axis=1) for ref in packet_refs]
    inner = lax.dot_general(
        joined(blocks, 0), observed_ref[...], (((1,), (1,)), ((), ())), preferred_element_type=jnp.float32
    )
    metas = [ref[panels * count :, :] for ref in packet_refs]
    after_steps = aux_ref.shape[0] - 2
    scale = aux_ref[after_steps : after_steps + 1, :]
    if first:
        top = jnp.full(scale.shape, NEG_START, jnp.float32)
    else:
        state_ref = refs[len(steps)]
        top = old = state_ref[0:1, :]
    scores = []
    for i, (step, block, meta) in enumerate(zip(steps, blocks, metas)):
        wide = block.astype(jnp.float32)
        half_square = 0.5 * jnp.sum(wide * wide, axis=1, keepdims=True)
        classes = meta[META_ROWS // 2 :].astype(jnp.float32)
        column = jnp.concatenate([classes] * (count // SUBLANES), axis=0).T[:, 0:1]
        active = column == aux_ref[step : step + 1, :]
        score = jnp.where(active, inner[i * count : (i + 1) * count] - half_square, -jnp.inf)
        top = jnp.maximum(top, jnp.max(score, axis=0, keepdims=True))
        scores.append(score)
    weights = [jnp.exp2((score - top) * scale) for score in scores]
    total = sum(jnp.sum(weight, axis=0, keepdims=True) for weight in weights)
    sums = lax.dot_general(
        joined(metas, 1), joined([weight.astype(jnp.bfloat16) for weight in weights], 0),
        (((1,), (0,)), ((), ())), preferred_element_type=jnp.float32,
    )[0:4]
    if not first:
        factor = jnp.exp2((old - top) * scale)
        total += state_ref[1:2, :] * factor
        sums += state_ref[2:6, :] * factor
    out_ref[0:1, :] = top
    out_ref[1:2, :] = total
    out_ref[2:6, :] = sums
    out_ref[6:8, :] = jnp.zeros_like(out_ref[6:8, :])


def finish_kernel(size, mine_ref, other_ref, aux_ref, mean_ref, evidence_ref):
    after_steps = aux_ref.shape[0] - 2
    scale = aux_ref[after_steps : after_steps + 1, :]
    top_a, top_b = mine_ref[0:1, :], other_ref[0:1, :]
    top = jnp.maximum(top_a, top_b)
    factor_a = jnp.exp2((top_a - top) * scale)
    factor_b = jnp.exp2((top_b - top) * scale)
    total = mine_ref[1:2, :] * factor_a + other_ref[1:2, :] * factor_b
    sums = mine_ref[2:6, :] * factor_a + other_ref[2:6, :] * factor_b
    mean_ref[...] = sums / total
    sharp = scale * (0.5 / LOG2E)
    evidence = sharp * (2.0 * size - aux_ref[after_steps + 1 : after_steps + 2, :] + 2.0 * top) + jnp.log(total)
    evidence_ref[...] = evidence.reshape(evidence_ref.shape)


def after(values, *earlier):
    return lax.optimization_barrier((values, earlier))[0]


def in_hbm(*arrays):
    return [pltpu.with_memory_space_constraint(array, pltpu.HBM) for array in arrays]


def on_device(pairs, block_of, observed, sharpness, obs_class, pattern, evolved, sim_params, sim_class):
    rows, size = observed.shape
    count = evolved.shape[0]
    devices = pattern.shape[1]
    steps = devices // 2
    vmem = pl.BlockSpec(memory_space=pltpu.VMEM)
    smem = pl.BlockSpec(memory_space=pltpu.SMEM)
    hbm = pl.BlockSpec(memory_space=pltpu.HBM)
    compiler_params = pltpu.CompilerParams(vmem_limit_bytes=VMEM_LIMIT)
    f32 = jnp.float32
    core = [(i, i ^ 1) for i in range(devices)]
    at = lax.axis_index("blk").astype(jnp.int32).reshape(1)

    packet = pl.pallas_call(
        pack_kernel,
        out_shape=jax.ShapeDtypeStruct((count * size // LANES + META_ROWS, LANES), evolved.dtype),
        in_specs=[hbm] * 3,
        out_specs=vmem,
        scratch_shapes=[
            pltpu.VMEM(sim_params.shape, sim_params.dtype),
            pltpu.VMEM(sim_class.shape, sim_class.dtype),
            pltpu.SemaphoreType.DMA((size // LANES + 2,)),
        ],
        compiler_params=compiler_params,
        name="pack",
    )(*in_hbm(sim_params, sim_class, evolved))
    packets = [packet]
    moving = [packet, packet]

    def send(step):
        kind = step % 2
        moving[kind] = lax.ppermute(moving[kind], "blk", pairs[(kind + step // 2) % 2])
        packets.append(moving[kind])

    send(0)
    own_aux, sib_aux, observed_own = pl.pallas_call(
        functools.partial(prepare_kernel, block_of),
        out_shape=(
            jax.ShapeDtypeStruct((steps + 2, rows), f32),
            jax.ShapeDtypeStruct((steps + 2, rows), f32),
            jax.ShapeDtypeStruct(observed.shape, observed.dtype),
        ),
        in_specs=[smem] + [hbm] * 4,
        out_specs=(vmem,) * 3,
        scratch_shapes=[
            pltpu.SMEM(pattern.shape, pattern.dtype),
            pltpu.VMEM(obs_class.shape, obs_class.dtype),
            pltpu.VMEM(sharpness.shape, sharpness.dtype),
            pltpu.SemaphoreType.DMA((4,)),
        ],
        compiler_params=compiler_params,
        cost_estimate=pl.CostEstimate(flops=8 * rows * size, bytes_accessed=4 * rows * size, transcendentals=0),
        name="prepare",
    )(after(at, packet), *in_hbm(pattern, obs_class, sharpness, observed))
    observed_sib = lax.ppermute(observed, "blk", core)
    sib_aux = lax.ppermute(sib_aux, "blk", core)
    moving[1] = after(moving[1], own_aux)
    send(1)

    def absorb(work, half, state):
        observed_half, aux = ((observed_own, own_aux), (observed_sib, sib_aux))[half]
        before = () if state is None else (state,)
        return pl.pallas_call(
            functools.partial(absorb_kernel, work, count, state is None),
            out_shape=jax.ShapeDtypeStruct((SUBLANES, rows), f32),
            in_specs=[vmem] * (2 + len(work) + len(before)),
            out_specs=vmem,
            compiler_params=compiler_params,
            cost_estimate=pl.CostEstimate(
                flops=2 * len(work) * rows * count * size,
                bytes_accessed=2 * (rows + len(work) * count) * size,
                transcendentals=len(work) * rows * count,
            ),
            name="absorb",
        )(observed_half, aux, *(packets[i] for i in work), *before)

    states = [None, None]
    works = []
    for first in range(0, steps, 2):
        work = tuple(range(first, min(first + 2, steps)))
        works += [(work, half) for half in ((0, 1) if first + 2 < steps else (1, 0))]
    done = []
    for step in range(steps - 1):
        ahead = step + 2
        if ahead < steps - 1:
            if done:
                moving[ahead % 2] = after(moving[ahead % 2], done[-1])
            send(ahead)
        if step < len(works):
            work, half = works[step]
            states[half] = absorb(work, half, states[half])
            done.append(states[half])
    for work, half in works[steps - 1 : -1]:
        states[half] = absorb(work, half, states[half])
    other = lax.ppermute(states[1], "blk", core)
    work, half = works[-1]
    states[half] = absorb(work, half, states[half])
    mean, evidence = pl.pallas_call(
        functools.partial(finish_kernel, size),
        out_shape=(jax.ShapeDtypeStruct((sim_params.shape[0], rows), f32), jax.ShapeDtypeStruct((rows,), f32)),
        in_specs=[vmem] * 3,
        out_specs=(vmem,) * 2,
        compiler_params=compiler_params,
        name="finish",
    )(states[0], other, own_aux)
    return mean, evidence


def solution(mesh):
    placed = (
        P(("parts", "blk"), None),
        P(("parts", "blk")),
        P(("parts", "blk")),
        P(("parts", "blk"), None),
        P(("parts", "blk"), None),
        P(None, ("parts", "blk")),
        P(("parts", "blk")),
    )
    pairs, block_of = plan(mesh.shape["blk"], mesh.shape["parts"] == 2)
    return jax.shard_map(
        functools.partial(on_device, pairs, block_of),
        mesh=mesh,
        in_specs=placed,
        out_specs=(P(None, ("parts", "blk")), P(("parts", "blk"))),
        check_vma=False,
    )
```

```python
import functools
import math

import jax
import jax.numpy as jnp
import numpy as np
from jax import lax
from jax.experimental import pallas as pl
from jax.experimental.pallas import tpu as pltpu
from jax.sharding import PartitionSpec as P

NEG_START = -1e30
LOG2E = math.log2(math.e)
SUBLANES = 8
LANES = 128
META_ROWS = 16
VMEM_LIMIT = 40 * 1024 * 1024


def plan(size, grid):
    chips = size // 2

    def ring(place):
        if not grid:
            return place
        return jnp.where(place < chips // 2, 2 * place, 2 * (chips - 1 - place) + 1)

    def place_of(chip):
        if not grid:
            return chip
        return jnp.where(chip % 2 == 0, chip // 2, chips - 1 - chip // 2)

    def beside(device, by):
        return ring((place_of(device // 2) + by + chips) % chips) * 2 + (device + by) % 2

    def block_of(device, step):
        if step == 0:
            return device
        stream, hop = (step - 1) % 2, (step - 1) // 2
        way = 1 - 2 * ((device + 1 + stream + hop) % 2)
        return beside(device, -way * (hop + 1))

    devices = np.arange(size)
    with jax.ensure_compile_time_eval():
        targets = [np.asarray(beside(devices, 1 - 2 * ((devices + parity) % 2))).tolist() for parity in range(2)]
    return [list(enumerate(target)) for target in targets], block_of


def joined(parts, axis):
    return parts[0] if len(parts) == 1 else jnp.concatenate(parts, axis=axis)


def row(values):
    return values.reshape(1, values.shape[-1])


def pack_kernel(params_hbm, class_hbm, evolved_hbm, packet_ref, meta_ref, params_ref, class_ref, arrived):
    rows, size = evolved_hbm.shape
    panels = size // LANES
    copies = [
        pltpu.make_async_copy(params_hbm, params_ref, arrived.at[0]),
        pltpu.make_async_copy(class_hbm, class_ref, arrived.at[1]),
    ]
    for i in range(panels):
        panel = packet_ref.at[pl.ds(i * rows, rows), :]
        source = evolved_hbm.at[:, pl.ds(i * LANES, LANES)]
        copies.append(pltpu.make_async_copy(source, panel, arrived.at[i + 2]))
    for copy in copies:
        copy.start()
    for copy in copies[:2]:
        copy.wait()
    params = params_ref[...].astype(jnp.float32)
    classes = row(class_ref[...]).astype(jnp.float32)
    rest = jnp.broadcast_to(classes, (META_ROWS - params.shape[0], classes.shape[1]))
    meta = jnp.concatenate([params, rest], axis=0).astype(packet_ref.dtype)
    packet_ref[panels * rows :, :] = meta
    meta_ref[...] = meta
    for copy in copies[2:]:
        copy.wait()


def join_kernel(block_ref, meta_ref, packet_ref):
    rows, size = block_ref.shape
    panels = size // LANES
    for i in range(panels):
        packet_ref[i * rows : (i + 1) * rows, :] = block_ref[:, i * LANES : (i + 1) * LANES]
    packet_ref[panels * rows :, :] = meta_ref[...]


def norms(observed):
    wide = observed.astype(jnp.float32)
    square = wide * wide
    high = square.astype(jnp.bfloat16)
    low = (square - high.astype(jnp.float32)).astype(jnp.bfloat16)
    ones = jnp.ones((SUBLANES, observed.shape[1]), jnp.bfloat16)
    return sum(
        lax.dot_general(ones, part, (((1,), (1,)), ((), ())), preferred_element_type=jnp.float32)[0:1]
        for part in (high, low)
    )


def prepare_kernel(
    block_of, at_ref, pattern_hbm, class_hbm, sharp_hbm, observed_hbm,
    own_ref, sib_ref, observed_ref, pattern_ref, class_ref, sharp_ref, arrived,
):
    sources = (pattern_hbm, class_hbm, sharp_hbm, observed_hbm)
    targets = (pattern_ref, class_ref, sharp_ref, observed_ref)
    copies = [
        pltpu.make_async_copy(source, target, arrived.at[i])
        for i, (source, target) in enumerate(zip(sources, targets))
    ]
    for copy in copies:
        copy.start()
    for copy in copies[:3]:
        copy.wait()
    tiles, devices = pattern_ref.shape
    tile = class_ref.shape[0] // tiles
    classes = row(class_ref[...]).astype(jnp.float32)
    scale = row(sharp_ref[...]) * (2.0 * LOG2E)
    for out_ref, device in ((own_ref, at_ref[0]), (sib_ref, at_ref[0] ^ 1)):
        for step in range(devices // 2):
            block = block_of(device, step)
            opened = [
                jnp.where(pattern_ref[i, block] == 1, classes[:, i * tile : (i + 1) * tile], -1.0) for i in range(tiles)
            ]
            out_ref[step : step + 1, :] = jnp.concatenate(opened, axis=1)
        out_ref[devices // 2 : devices // 2 + 1, :] = scale
    copies[3].wait()
    own_ref[devices // 2 + 1 : devices // 2 + 2, :] = norms(observed_ref[...])
    sib_ref[devices // 2 + 1 : devices // 2 + 2, :] = scale


def absorb_kernel(steps, count, first, observed_ref, aux_ref, *refs):
    packet_refs, out_ref = refs[: len(steps)], refs[-1]
    panels = observed_ref.shape[1] // LANES
    blocks = [jnp.concatenate([ref[i * count : (i + 1) * count, :] for i in range(panels)], axis=1) for ref in packet_refs]
    inner = lax.dot_general(
        joined(blocks, 0), observed_ref[...], (((1,), (1,)), ((), ())), preferred_element_type=jnp.float32
    )
    metas = [ref[panels * count :, :] for ref in packet_refs]
    after_steps = aux_ref.shape[0] - 2
    scale = aux_ref[after_steps : after_steps + 1, :]
    if first:
        top = jnp.full(scale.shape, NEG_START, jnp.float32)
    else:
        state_ref = refs[len(steps)]
        top = old = state_ref[0:1, :]
    scores = []
    for i, (step, block, meta) in enumerate(zip(steps, blocks, metas)):
        wide = block.astype(jnp.float32)
        half_square = 0.5 * jnp.sum(wide * wide, axis=1, keepdims=True)
        classes = meta[META_ROWS // 2 :].astype(jnp.float32)
        column = jnp.concatenate([classes] * (count // SUBLANES), axis=0).T[:, 0:1]
        active = column == aux_ref[step : step + 1, :]
        score = jnp.where(active, inner[i * count : (i + 1) * count] - half_square, -jnp.inf)
        top = jnp.maximum(top, jnp.max(score, axis=0, keepdims=True))
        scores.append(score)
    weights = [jnp.exp2((score - top) * scale) for score in scores]
    total = sum(jnp.sum(weight, axis=0, keepdims=True) for weight in weights)
    sums = lax.dot_general(
        joined(metas, 1), joined([weight.astype(jnp.bfloat16) for weight in weights], 0),
        (((1,), (0,)), ((), ())), preferred_element_type=jnp.float32,
    )[0:4]
    if not first:
        factor = jnp.exp2((old - top) * scale)
        total += state_ref[1:2, :] * factor
        sums += state_ref[2:6, :] * factor
    out_ref[0:1, :] = top
    out_ref[1:2, :] = total
    out_ref[2:6, :] = sums
    out_ref[6:8, :] = jnp.zeros_like(out_ref[6:8, :])


def finish_kernel(size, mine_ref, other_ref, aux_ref, mean_ref, evidence_ref):
    after_steps = aux_ref.shape[0] - 2
    scale = aux_ref[after_steps : after_steps + 1, :]
    top_a, top_b = mine_ref[0:1, :], other_ref[0:1, :]
    top = jnp.maximum(top_a, top_b)
    factor_a = jnp.exp2((top_a - top) * scale)
    factor_b = jnp.exp2((top_b - top) * scale)
    total = mine_ref[1:2, :] * factor_a + other_ref[1:2, :] * factor_b
    sums = mine_ref[2:6, :] * factor_a + other_ref[2:6, :] * factor_b
    mean_ref[...] = sums / total
    sharp = scale * (0.5 / LOG2E)
    evidence = sharp * (2.0 * size - aux_ref[after_steps + 1 : after_steps + 2, :] + 2.0 * top) + jnp.log(total)
    evidence_ref[...] = evidence.reshape(evidence_ref.shape)


def after(values, *earlier):
    return lax.optimization_barrier((values, earlier))[0]


def in_hbm(*arrays):
    return [pltpu.with_memory_space_constraint(array, pltpu.HBM) for array in arrays]


def cost(microseconds):
    return pl.CostEstimate(flops=int(microseconds * 1.15e9), bytes_accessed=0, transcendentals=0)


def on_device(pairs, block_of, observed, sharpness, obs_class, pattern, evolved, sim_params, sim_class):
    rows, size = observed.shape
    count = evolved.shape[0]
    devices = pattern.shape[1]
    steps = devices // 2
    vmem = pl.BlockSpec(memory_space=pltpu.VMEM)
    smem = pl.BlockSpec(memory_space=pltpu.SMEM)
    hbm = pl.BlockSpec(memory_space=pltpu.HBM)
    compiler_params = pltpu.CompilerParams(vmem_limit_bytes=VMEM_LIMIT)
    f32 = jnp.float32
    core = [(i, i ^ 1) for i in range(devices)]
    at = lax.axis_index("blk").astype(jnp.int32).reshape(1)

    first = lax.ppermute(evolved, "blk", pairs[0])
    packet, meta = pl.pallas_call(
        pack_kernel,
        out_shape=(
            jax.ShapeDtypeStruct((count * size // LANES + META_ROWS, LANES), evolved.dtype),
            jax.ShapeDtypeStruct((META_ROWS, LANES), evolved.dtype),
        ),
        in_specs=[hbm] * 3,
        out_specs=(vmem,) * 2,
        scratch_shapes=[
            pltpu.VMEM(sim_params.shape, sim_params.dtype),
            pltpu.VMEM(sim_class.shape, sim_class.dtype),
            pltpu.SemaphoreType.DMA((size // LANES + 2,)),
        ],
        compiler_params=compiler_params,
        cost_estimate=cost(0.05),
        name="pack",
    )(*in_hbm(sim_params, sim_class, evolved))
    first_meta = lax.ppermute(meta, "blk", pairs[0])
    own_aux, sib_aux, observed_own = pl.pallas_call(
        functools.partial(prepare_kernel, block_of),
        out_shape=(
            jax.ShapeDtypeStruct((steps + 2, rows), f32),
            jax.ShapeDtypeStruct((steps + 2, rows), f32),
            jax.ShapeDtypeStruct(observed.shape, observed.dtype),
        ),
        in_specs=[smem] + [hbm] * 4,
        out_specs=(vmem,) * 3,
        scratch_shapes=[
            pltpu.SMEM(pattern.shape, pattern.dtype),
            pltpu.VMEM(obs_class.shape, obs_class.dtype),
            pltpu.VMEM(sharpness.shape, sharpness.dtype),
            pltpu.SemaphoreType.DMA((4,)),
        ],
        compiler_params=compiler_params,
        cost_estimate=cost(0.05),
        name="prepare",
    )(after(at, packet), *in_hbm(pattern, obs_class, sharpness, observed))
    observed_sib = lax.ppermute(observed, "blk", core)
    sib_aux = lax.ppermute(sib_aux, "blk", core)
    packets = [packet]
    moving = [None, after(packet, first_meta, own_aux)]

    def send(step):
        kind = step % 2
        moving[kind] = lax.ppermute(moving[kind], "blk", pairs[(kind + step // 2) % 2])
        packets.append(moving[kind])

    moving[0] = pl.pallas_call(
        join_kernel,
        out_shape=jax.ShapeDtypeStruct(packet.shape, packet.dtype),
        in_specs=[vmem] * 2,
        out_specs=vmem,
        compiler_params=compiler_params,
        cost_estimate=cost(0.1),
        name="join",
    )(first, first_meta)
    packets.append(moving[0])
    send(1)

    def absorb(work, half, state):
        observed_half, aux = ((observed_own, own_aux), (observed_sib, sib_aux))[half]
        before = () if state is None else (state,)
        return pl.pallas_call(
            functools.partial(absorb_kernel, work, count, state is None),
            out_shape=jax.ShapeDtypeStruct((SUBLANES, rows), f32),
            in_specs=[vmem] * (2 + len(work) + len(before)),
            out_specs=vmem,
            compiler_params=compiler_params,
            cost_estimate=cost(0.1),
            name="absorb",
        )(observed_half, aux, *(packets[i] for i in work), *before)

    works = [[] for _ in range(steps)]
    waiting = ()
    for block in range(1, steps - 2, 2):
        works[block - 1] += [(waiting, 1)] if waiting else []
        works[block - 1].append(((block - 1, block), 0))
        waiting = (block - 1, block)
    works[steps - 3] += [((*waiting, steps - 2), 1), ((steps - 2,), 0)]
    works[steps - 2] += [((steps - 1,), 1), ((steps - 1,), 0)]
    states = [None, None]
    done = []
    for step in range(steps - 1):
        ahead = step + 2
        if ahead < steps - 1:
            if done:
                moving[ahead % 2] = after(moving[ahead % 2], *done[-2:])
            send(ahead)
        last = step == steps - 2
        if last:
            packets[-1] = after(packets[-1], states[0], states[1])
        for work, half in works[step]:
            states[half] = absorb(work, half, states[half])
            done.append(states[half])
            if last and half == 1:
                other = lax.ppermute(states[1], "blk", core)
    mean, evidence = pl.pallas_call(
        functools.partial(finish_kernel, size),
        out_shape=(jax.ShapeDtypeStruct((sim_params.shape[0], rows), f32), jax.ShapeDtypeStruct((rows,), f32)),
        in_specs=[vmem] * 3,
        out_specs=(vmem,) * 2,
        compiler_params=compiler_params,
        name="finish",
    )(states[0], other, own_aux)
    return mean, evidence


def solution(mesh):
    placed = (
        P(("parts", "blk"), None),
        P(("parts", "blk")),
        P(("parts", "blk")),
        P(("parts", "blk"), None),
        P(("parts", "blk"), None),
        P(None, ("parts", "blk")),
        P(("parts", "blk")),
    )
    pairs, block_of = plan(mesh.shape["blk"], mesh.shape["parts"] == 2)
    return jax.shard_map(
        functools.partial(on_device, pairs, block_of),
        mesh=mesh,
        in_specs=placed,
        out_specs=(P(None, ("parts", "blk")), P(("parts", "blk"))),
        check_vma=False,
    )
```

```python
import functools
import math

import jax
import jax.numpy as jnp
import numpy as np
from jax import lax
from jax.experimental import pallas as pl
from jax.experimental.pallas import tpu as pltpu
from jax.sharding import PartitionSpec as P

NEG_START = -1e30
LOG2E = math.log2(math.e)
SUBLANES = 8
LANES = 128
META_ROWS = 16
VMEM_LIMIT = 40 * 1024 * 1024


def plan(size, grid):
    chips = size // 2

    def ring(place):
        if not grid:
            return place
        return jnp.where(place < chips // 2, 2 * place, 2 * (chips - 1 - place) + 1)

    def place_of(chip):
        if not grid:
            return chip
        return jnp.where(chip % 2 == 0, chip // 2, chips - 1 - chip // 2)

    def beside(device, by):
        return ring((place_of(device // 2) + by + chips) % chips) * 2 + (device + by) % 2

    def block_of(device, step):
        if step == 0:
            return device
        stream, hop = (step - 1) % 2, (step - 1) // 2
        way = 1 - 2 * ((device + 1 + stream + hop) % 2)
        return beside(device, -way * (hop + 1))

    devices = np.arange(size)
    with jax.ensure_compile_time_eval():
        targets = [np.asarray(beside(devices, 1 - 2 * ((devices + parity) % 2))).tolist() for parity in range(2)]
    return [list(enumerate(target)) for target in targets], block_of


def joined(parts, axis):
    return parts[0] if len(parts) == 1 else jnp.concatenate(parts, axis=axis)


def row(values):
    return values.reshape(1, values.shape[-1])


def pack_kernel(params_hbm, class_hbm, evolved_hbm, packet_ref, params_ref, class_ref, arrived):
    rows, size = evolved_hbm.shape
    panels = size // LANES
    copies = [
        pltpu.make_async_copy(params_hbm, params_ref, arrived.at[0]),
        pltpu.make_async_copy(class_hbm, class_ref, arrived.at[1]),
    ]
    for i in range(panels):
        panel = packet_ref.at[pl.ds(i * rows, rows), :]
        source = evolved_hbm.at[:, pl.ds(i * LANES, LANES)]
        copies.append(pltpu.make_async_copy(source, panel, arrived.at[i + 2]))
    for copy in copies:
        copy.start()
    for copy in copies[:2]:
        copy.wait()
    params = params_ref[...].astype(jnp.float32)
    classes = row(class_ref[...]).astype(jnp.float32)
    rest = jnp.broadcast_to(classes, (META_ROWS - params.shape[0], classes.shape[1]))
    packet_ref[panels * rows :, :] = jnp.concatenate([params, rest], axis=0).astype(packet_ref.dtype)
    for copy in copies[2:]:
        copy.wait()


def norms(observed):
    wide = observed.astype(jnp.float32)
    square = wide * wide
    high = square.astype(jnp.bfloat16)
    low = (square - high.astype(jnp.float32)).astype(jnp.bfloat16)
    ones = jnp.ones((SUBLANES, observed.shape[1]), jnp.bfloat16)
    return sum(
        lax.dot_general(ones, part, (((1,), (1,)), ((), ())), preferred_element_type=jnp.float32)[0:1]
        for part in (high, low)
    )


def prepare_kernel(
    block_of, at_ref, pattern_hbm, class_hbm, sharp_hbm, observed_hbm,
    own_ref, sib_ref, observed_ref, pattern_ref, class_ref, sharp_ref, arrived,
):
    sources = (pattern_hbm, class_hbm, sharp_hbm, observed_hbm)
    targets = (pattern_ref, class_ref, sharp_ref, observed_ref)
    copies = [
        pltpu.make_async_copy(source, target, arrived.at[i])
        for i, (source, target) in enumerate(zip(sources, targets))
    ]
    for copy in copies:
        copy.start()
    for copy in copies[:3]:
        copy.wait()
    tiles, devices = pattern_ref.shape
    tile = class_ref.shape[0] // tiles
    classes = row(class_ref[...]).astype(jnp.float32)
    scale = row(sharp_ref[...]) * (2.0 * LOG2E)
    for out_ref, device in ((own_ref, at_ref[0]), (sib_ref, at_ref[0] ^ 1)):
        for step in range(devices // 2):
            block = block_of(device, step)
            opened = [
                jnp.where(pattern_ref[i, block] == 1, classes[:, i * tile : (i + 1) * tile], -1.0) for i in range(tiles)
            ]
            out_ref[step : step + 1, :] = jnp.concatenate(opened, axis=1)
        out_ref[devices // 2 : devices // 2 + 1, :] = scale
    copies[3].wait()
    own_ref[devices // 2 + 1 : devices // 2 + 2, :] = norms(observed_ref[...])
    sib_ref[devices // 2 + 1 : devices // 2 + 2, :] = scale


def absorb_kernel(steps, count, first, observed_ref, aux_ref, *refs):
    packet_refs, out_ref = refs[: len(steps)], refs[-1]
    panels = observed_ref.shape[1] // LANES
    blocks = [jnp.concatenate([ref[i * count : (i + 1) * count, :] for i in range(panels)], axis=1) for ref in packet_refs]
    inner = lax.dot_general(
        joined(blocks, 0), observed_ref[...], (((1,), (1,)), ((), ())), preferred_element_type=jnp.float32
    )
    metas = [ref[panels * count :, :] for ref in packet_refs]
    after_steps = aux_ref.shape[0] - 2
    scale = aux_ref[after_steps : after_steps + 1, :]
    if first:
        top = jnp.full(scale.shape, NEG_START, jnp.float32)
    else:
        state_ref = refs[len(steps)]
        top = old = state_ref[0:1, :]
    scores = []
    for i, (step, block, meta) in enumerate(zip(steps, blocks, metas)):
        wide = block.astype(jnp.float32)
        half_square = 0.5 * jnp.sum(wide * wide, axis=1, keepdims=True)
        classes = meta[META_ROWS // 2 :].astype(jnp.float32)
        column = jnp.concatenate([classes] * (count // SUBLANES), axis=0).T[:, 0:1]
        active = column == aux_ref[step : step + 1, :]
        score = jnp.where(active, inner[i * count : (i + 1) * count] - half_square, -jnp.inf)
        top = jnp.maximum(top, jnp.max(score, axis=0, keepdims=True))
        scores.append(score)
    weights = [jnp.exp2((score - top) * scale) for score in scores]
    total = sum(jnp.sum(weight, axis=0, keepdims=True) for weight in weights)
    sums = lax.dot_general(
        joined(metas, 1), joined([weight.astype(jnp.bfloat16) for weight in weights], 0),
        (((1,), (0,)), ((), ())), preferred_element_type=jnp.float32,
    )[0:4]
    if not first:
        factor = jnp.exp2((old - top) * scale)
        total += state_ref[1:2, :] * factor
        sums += state_ref[2:6, :] * factor
    out_ref[0:1, :] = top
    out_ref[1:2, :] = total
    out_ref[2:6, :] = sums
    out_ref[6:8, :] = jnp.zeros_like(out_ref[6:8, :])


def finish_kernel(size, mine_ref, other_ref, aux_ref, mean_ref, evidence_ref):
    after_steps = aux_ref.shape[0] - 2
    scale = aux_ref[after_steps : after_steps + 1, :]
    top_a, top_b = mine_ref[0:1, :], other_ref[0:1, :]
    top = jnp.maximum(top_a, top_b)
    factor_a = jnp.exp2((top_a - top) * scale)
    factor_b = jnp.exp2((top_b - top) * scale)
    total = mine_ref[1:2, :] * factor_a + other_ref[1:2, :] * factor_b
    sums = mine_ref[2:6, :] * factor_a + other_ref[2:6, :] * factor_b
    mean_ref[...] = sums / total
    sharp = scale * (0.5 / LOG2E)
    evidence = sharp * (2.0 * size - aux_ref[after_steps + 1 : after_steps + 2, :] + 2.0 * top) + jnp.log(total)
    evidence_ref[...] = evidence.reshape(evidence_ref.shape)


def after(values, *earlier):
    return lax.optimization_barrier((values, earlier))[0]


def in_hbm(*arrays):
    return [pltpu.with_memory_space_constraint(array, pltpu.HBM) for array in arrays]


def on_device(pairs, block_of, observed, sharpness, obs_class, pattern, evolved, sim_params, sim_class):
    rows, size = observed.shape
    count = evolved.shape[0]
    devices = pattern.shape[1]
    steps = devices // 2
    vmem = pl.BlockSpec(memory_space=pltpu.VMEM)
    smem = pl.BlockSpec(memory_space=pltpu.SMEM)
    hbm = pl.BlockSpec(memory_space=pltpu.HBM)
    compiler_params = pltpu.CompilerParams(vmem_limit_bytes=VMEM_LIMIT)
    f32 = jnp.float32
    core = [(i, i ^ 1) for i in range(devices)]
    at = lax.axis_index("blk").astype(jnp.int32).reshape(1)

    packet = pl.pallas_call(
        pack_kernel,
        out_shape=jax.ShapeDtypeStruct((count * size // LANES + META_ROWS, LANES), evolved.dtype),
        in_specs=[hbm] * 3,
        out_specs=vmem,
        scratch_shapes=[
            pltpu.VMEM(sim_params.shape, sim_params.dtype),
            pltpu.VMEM(sim_class.shape, sim_class.dtype),
            pltpu.SemaphoreType.DMA((size // LANES + 2,)),
        ],
        compiler_params=compiler_params,
        name="pack",
    )(*in_hbm(sim_params, sim_class, evolved))
    packets = [packet]
    moving = [packet, packet]

    def send(step):
        kind = step % 2
        moving[kind] = lax.ppermute(moving[kind], "blk", pairs[(kind + step // 2) % 2])
        packets.append(moving[kind])

    send(0)
    own_aux, sib_aux, observed_own = pl.pallas_call(
        functools.partial(prepare_kernel, block_of),
        out_shape=(
            jax.ShapeDtypeStruct((steps + 2, rows), f32),
            jax.ShapeDtypeStruct((steps + 2, rows), f32),
            jax.ShapeDtypeStruct(observed.shape, observed.dtype),
        ),
        in_specs=[smem] + [hbm] * 4,
        out_specs=(vmem,) * 3,
        scratch_shapes=[
            pltpu.SMEM(pattern.shape, pattern.dtype),
            pltpu.VMEM(obs_class.shape, obs_class.dtype),
            pltpu.VMEM(sharpness.shape, sharpness.dtype),
            pltpu.SemaphoreType.DMA((4,)),
        ],
        compiler_params=compiler_params,
        cost_estimate=pl.CostEstimate(flops=8 * rows * size, bytes_accessed=4 * rows * size, transcendentals=0),
        name="prepare",
    )(after(at, packet), *in_hbm(pattern, obs_class, sharpness, observed))
    observed_sib = lax.ppermute(observed, "blk", core)
    sib_aux = lax.ppermute(sib_aux, "blk", core)
    moving[1] = after(moving[1], own_aux)
    send(1)

    def absorb(work, half, state):
        observed_half, aux = ((observed_own, own_aux), (observed_sib, sib_aux))[half]
        before = () if state is None else (state,)
        return pl.pallas_call(
            functools.partial(absorb_kernel, work, count, state is None),
            out_shape=jax.ShapeDtypeStruct((SUBLANES, rows), f32),
            in_specs=[vmem] * (2 + len(work) + len(before)),
            out_specs=vmem,
            compiler_params=compiler_params,
            cost_estimate=pl.CostEstimate(
                flops=2 * len(work) * rows * count * size,
                bytes_accessed=2 * (rows + len(work) * count) * size,
                transcendentals=len(work) * rows * count,
            ),
            name="absorb",
        )(observed_half, aux, *(packets[i] for i in work), *before)

    works = [[] for _ in range(steps)]
    for block in range(1, steps - 2, 2):
        works[block - 1].append(((block - 1, block), 0))
        works[block].append(((block - 1, block), 1))
    works[steps - 3] += [((steps - 2,), 0), ((steps - 2,), 1)]
    works[steps - 2] += [((steps - 1,), 1), ((steps - 1,), 0)]
    states = [None, None]
    done = []
    for step in range(steps - 1):
        ahead = step + 2
        if ahead < steps - 1:
            if done:
                moving[ahead % 2] = after(moving[ahead % 2], done[-1])
            send(ahead)
        last = step == steps - 2
        if last:
            packets[-1] = after(packets[-1], states[0], states[1])
        for work, half in works[step]:
            states[half] = absorb(work, half, states[half])
            done.append(states[half])
            if last and half == 1:
                other = lax.ppermute(states[1], "blk", core)
    mean, evidence = pl.pallas_call(
        functools.partial(finish_kernel, size),
        out_shape=(jax.ShapeDtypeStruct((sim_params.shape[0], rows), f32), jax.ShapeDtypeStruct((rows,), f32)),
        in_specs=[vmem] * 3,
        out_specs=(vmem,) * 2,
        compiler_params=compiler_params,
        name="finish",
    )(states[0], other, own_aux)
    return mean, evidence


def solution(mesh):
    placed = (
        P(("parts", "blk"), None),
        P(("parts", "blk")),
        P(("parts", "blk")),
        P(("parts", "blk"), None),
        P(("parts", "blk"), None),
        P(None, ("parts", "blk")),
        P(("parts", "blk")),
    )
    pairs, block_of = plan(mesh.shape["blk"], mesh.shape["parts"] == 2)
    return jax.shard_map(
        functools.partial(on_device, pairs, block_of),
        mesh=mesh,
        in_specs=placed,
        out_specs=(P(None, ("parts", "blk")), P(("parts", "blk"))),
        check_vma=False,
    )
```

```python
import functools
import math

import jax
import jax.numpy as jnp
import numpy as np
from jax import lax
from jax.experimental import pallas as pl
from jax.experimental.pallas import tpu as pltpu
from jax.sharding import PartitionSpec as P

NEG_START = -1e30
LOG2E = math.log2(math.e)
SUBLANES = 8
LANES = 128
META_ROWS = 16
VMEM_LIMIT = 40 * 1024 * 1024


def plan(size, grid):
    chips = size // 2

    def ring(place):
        if not grid:
            return place
        return jnp.where(place < chips // 2, 2 * place, 2 * (chips - 1 - place) + 1)

    def place_of(chip):
        if not grid:
            return chip
        return jnp.where(chip % 2 == 0, chip // 2, chips - 1 - chip // 2)

    def beside(device, by):
        return ring((place_of(device // 2) + by + chips) % chips) * 2 + (device + by) % 2

    def block_of(device, step):
        if step == 0:
            return device
        stream, hop = (step - 1) % 2, (step - 1) // 2
        way = 1 - 2 * ((device + 1 + stream + hop) % 2)
        return beside(device, -way * (hop + 1))

    devices = np.arange(size)
    with jax.ensure_compile_time_eval():
        targets = [np.asarray(beside(devices, 1 - 2 * ((devices + parity) % 2))).tolist() for parity in range(2)]
    return [list(enumerate(target)) for target in targets], block_of


def joined(parts, axis):
    return parts[0] if len(parts) == 1 else jnp.concatenate(parts, axis=axis)


def row(values):
    return values.reshape(1, values.shape[-1])


def pack_kernel(params_hbm, class_hbm, evolved_hbm, packet_ref, params_ref, class_ref, arrived):
    rows, size = evolved_hbm.shape
    panels = size // LANES
    copies = [
        pltpu.make_async_copy(params_hbm, params_ref, arrived.at[0]),
        pltpu.make_async_copy(class_hbm, class_ref, arrived.at[1]),
    ]
    for i in range(panels):
        panel = packet_ref.at[pl.ds(i * rows, rows), :]
        source = evolved_hbm.at[:, pl.ds(i * LANES, LANES)]
        copies.append(pltpu.make_async_copy(source, panel, arrived.at[i + 2]))
    for copy in copies:
        copy.start()
    for copy in copies[:2]:
        copy.wait()
    params = params_ref[...].astype(jnp.float32)
    classes = row(class_ref[...]).astype(jnp.float32)
    rest = jnp.broadcast_to(classes, (META_ROWS - params.shape[0], classes.shape[1]))
    packet_ref[panels * rows :, :] = jnp.concatenate([params, rest], axis=0).astype(packet_ref.dtype)
    for copy in copies[2:]:
        copy.wait()


def norms(observed):
    wide = observed.astype(jnp.float32)
    square = wide * wide
    high = square.astype(jnp.bfloat16)
    low = (square - high.astype(jnp.float32)).astype(jnp.bfloat16)
    ones = jnp.ones((SUBLANES, observed.shape[1]), jnp.bfloat16)
    return sum(
        lax.dot_general(ones, part, (((1,), (1,)), ((), ())), preferred_element_type=jnp.float32)[0:1]
        for part in (high, low)
    )


def prepare_kernel(
    block_of, at_ref, pattern_hbm, class_hbm, sharp_hbm, observed_hbm,
    own_ref, sib_ref, observed_ref, pattern_ref, class_ref, sharp_ref, arrived,
):
    sources = (pattern_hbm, class_hbm, sharp_hbm, observed_hbm)
    targets = (pattern_ref, class_ref, sharp_ref, observed_ref)
    copies = [
        pltpu.make_async_copy(source, target, arrived.at[i])
        for i, (source, target) in enumerate(zip(sources, targets))
    ]
    for copy in copies:
        copy.start()
    for copy in copies[:3]:
        copy.wait()
    tiles, devices = pattern_ref.shape
    tile = class_ref.shape[0] // tiles
    classes = row(class_ref[...]).astype(jnp.float32)
    scale = row(sharp_ref[...]) * (2.0 * LOG2E)
    for out_ref, device in ((own_ref, at_ref[0]), (sib_ref, at_ref[0] ^ 1)):
        for step in range(devices // 2):
            block = block_of(device, step)
            opened = [
                jnp.where(pattern_ref[i, block] == 1, classes[:, i * tile : (i + 1) * tile], -1.0) for i in range(tiles)
            ]
            out_ref[step : step + 1, :] = jnp.concatenate(opened, axis=1)
        out_ref[devices // 2 : devices // 2 + 1, :] = scale
    copies[3].wait()
    own_ref[devices // 2 + 1 : devices // 2 + 2, :] = norms(observed_ref[...])
    sib_ref[devices // 2 + 1 : devices // 2 + 2, :] = scale


def absorb_kernel(steps, count, first, observed_ref, aux_ref, *refs):
    packet_refs, out_ref = refs[: len(steps)], refs[-1]
    panels = observed_ref.shape[1] // LANES
    blocks = [jnp.concatenate([ref[i * count : (i + 1) * count, :] for i in range(panels)], axis=1) for ref in packet_refs]
    inner = lax.dot_general(
        joined(blocks, 0), observed_ref[...], (((1,), (1,)), ((), ())), preferred_element_type=jnp.float32
    )
    metas = [ref[panels * count :, :] for ref in packet_refs]
    after_steps = aux_ref.shape[0] - 2
    scale = aux_ref[after_steps : after_steps + 1, :]
    if first:
        top = jnp.full(scale.shape, NEG_START, jnp.float32)
    else:
        state_ref = refs[len(steps)]
        top = old = state_ref[0:1, :]
    scores = []
    for i, (step, block, meta) in enumerate(zip(steps, blocks, metas)):
        wide = block.astype(jnp.float32)
        half_square = 0.5 * jnp.sum(wide * wide, axis=1, keepdims=True)
        classes = meta[META_ROWS // 2 :].astype(jnp.float32)
        column = jnp.concatenate([classes] * (count // SUBLANES), axis=0).T[:, 0:1]
        active = column == aux_ref[step : step + 1, :]
        score = jnp.where(active, inner[i * count : (i + 1) * count] - half_square, -jnp.inf)
        top = jnp.maximum(top, jnp.max(score, axis=0, keepdims=True))
        scores.append(score)
    weights = [jnp.exp2((score - top) * scale) for score in scores]
    total = sum(jnp.sum(weight, axis=0, keepdims=True) for weight in weights)
    sums = lax.dot_general(
        joined(metas, 1), joined([weight.astype(jnp.bfloat16) for weight in weights], 0),
        (((1,), (0,)), ((), ())), preferred_element_type=jnp.float32,
    )[0:4]
    if not first:
        factor = jnp.exp2((old - top) * scale)
        total += state_ref[1:2, :] * factor
        sums += state_ref[2:6, :] * factor
    out_ref[0:1, :] = top
    out_ref[1:2, :] = total
    out_ref[2:6, :] = sums
    out_ref[6:8, :] = jnp.zeros_like(out_ref[6:8, :])


def finish_kernel(size, mine_ref, other_ref, aux_ref, mean_ref, evidence_ref):
    after_steps = aux_ref.shape[0] - 2
    scale = aux_ref[after_steps : after_steps + 1, :]
    top_a, top_b = mine_ref[0:1, :], other_ref[0:1, :]
    top = jnp.maximum(top_a, top_b)
    factor_a = jnp.exp2((top_a - top) * scale)
    factor_b = jnp.exp2((top_b - top) * scale)
    total = mine_ref[1:2, :] * factor_a + other_ref[1:2, :] * factor_b
    sums = mine_ref[2:6, :] * factor_a + other_ref[2:6, :] * factor_b
    mean_ref[...] = sums / total
    sharp = scale * (0.5 / LOG2E)
    evidence = sharp * (2.0 * size - aux_ref[after_steps + 1 : after_steps + 2, :] + 2.0 * top) + jnp.log(total)
    evidence_ref[...] = evidence.reshape(evidence_ref.shape)


def after(values, *earlier):
    return lax.optimization_barrier((values, earlier))[0]


def in_hbm(*arrays):
    return [pltpu.with_memory_space_constraint(array, pltpu.HBM) for array in arrays]


def on_device(pairs, block_of, observed, sharpness, obs_class, pattern, evolved, sim_params, sim_class):
    rows, size = observed.shape
    count = evolved.shape[0]
    devices = pattern.shape[1]
    steps = devices // 2
    vmem = pl.BlockSpec(memory_space=pltpu.VMEM)
    smem = pl.BlockSpec(memory_space=pltpu.SMEM)
    hbm = pl.BlockSpec(memory_space=pltpu.HBM)
    compiler_params = pltpu.CompilerParams(vmem_limit_bytes=VMEM_LIMIT)
    f32 = jnp.float32
    core = [(i, i ^ 1) for i in range(devices)]
    at = lax.axis_index("blk").astype(jnp.int32).reshape(1)

    packet = pl.pallas_call(
        pack_kernel,
        out_shape=jax.ShapeDtypeStruct((count * size // LANES + META_ROWS, LANES), evolved.dtype),
        in_specs=[hbm] * 3,
        out_specs=vmem,
        scratch_shapes=[
            pltpu.VMEM(sim_params.shape, sim_params.dtype),
            pltpu.VMEM(sim_class.shape, sim_class.dtype),
            pltpu.SemaphoreType.DMA((size // LANES + 2,)),
        ],
        compiler_params=compiler_params,
        name="pack",
    )(*in_hbm(sim_params, sim_class, evolved))
    packets = [packet]
    moving = [packet, packet]

    def send(step):
        kind = step % 2
        moving[kind] = lax.ppermute(moving[kind], "blk", pairs[(kind + step // 2) % 2])
        packets.append(moving[kind])

    send(0)
    own_aux, sib_aux, observed_own = pl.pallas_call(
        functools.partial(prepare_kernel, block_of),
        out_shape=(
            jax.ShapeDtypeStruct((steps + 2, rows), f32),
            jax.ShapeDtypeStruct((steps + 2, rows), f32),
            jax.ShapeDtypeStruct(observed.shape, observed.dtype),
        ),
        in_specs=[smem] + [hbm] * 4,
        out_specs=(vmem,) * 3,
        scratch_shapes=[
            pltpu.SMEM(pattern.shape, pattern.dtype),
            pltpu.VMEM(obs_class.shape, obs_class.dtype),
            pltpu.VMEM(sharpness.shape, sharpness.dtype),
            pltpu.SemaphoreType.DMA((4,)),
        ],
        compiler_params=compiler_params,
        cost_estimate=pl.CostEstimate(flops=8 * rows * size, bytes_accessed=4 * rows * size, transcendentals=0),
        name="prepare",
    )(after(at, packet), *in_hbm(pattern, obs_class, sharpness, observed))
    observed_sib = lax.ppermute(observed, "blk", core)
    sib_aux = lax.ppermute(sib_aux, "blk", core)
    moving[1] = after(moving[1], own_aux)
    send(1)

    def absorb(work, half, state):
        observed_half, aux = (observed_sib, sib_aux) if half else (observed_own, own_aux)
        before = () if state is None else (state,)
        return pl.pallas_call(
            functools.partial(absorb_kernel, work, count, state is None),
            out_shape=jax.ShapeDtypeStruct((SUBLANES, rows), f32),
            in_specs=[vmem] * (2 + len(work) + len(before)),
            out_specs=vmem,
            compiler_params=compiler_params,
            cost_estimate=pl.CostEstimate(
                flops=2 * len(work) * rows * count * size,
                bytes_accessed=2 * (rows + len(work) * count) * size,
                transcendentals=len(work) * rows * count,
            ),
            name="absorb",
        )(observed_half, aux, *(packets[i] for i in work), *before)

    works = [[] for _ in range(steps)]
    for block in range(1, steps - 2, 2):
        works[block - 1].append(((block - 1, block), 0))
        works[block].append(((block - 1, block), 1))
    works[steps - 3] += [((steps - 2,), 0), ((steps - 2,), 1)]
    works[steps - 2] += [((steps - 1,), 1), ((steps - 1,), 0)]
    states = [None, None]
    done = []
    for step in range(steps - 1):
        ahead = step + 2
        if ahead < steps - 1:
            if done:
                moving[ahead % 2] = after(moving[ahead % 2], done[-1])
            send(ahead)
        last = step == steps - 2
        if last:
            packets[-1] = after(packets[-1], states[0], states[1])
        if step == 0:
            own_aux = after(own_aux, sib_aux)
        for work, half in works[step]:
            states[half] = absorb(work, half, states[half])
            done.append(states[half])
            if last and half == 1:
                other = lax.ppermute(states[1], "blk", core)
    mean, evidence = pl.pallas_call(
        functools.partial(finish_kernel, size),
        out_shape=(jax.ShapeDtypeStruct((sim_params.shape[0], rows), f32), jax.ShapeDtypeStruct((rows,), f32)),
        in_specs=[vmem] * 3,
        out_specs=(vmem,) * 2,
        compiler_params=compiler_params,
        name="finish",
    )(states[0], other, own_aux)
    return mean, evidence


def solution(mesh):
    placed = (
        P(("parts", "blk"), None),
        P(("parts", "blk")),
        P(("parts", "blk")),
        P(("parts", "blk"), None),
        P(("parts", "blk"), None),
        P(None, ("parts", "blk")),
        P(("parts", "blk")),
    )
    pairs, block_of = plan(mesh.shape["blk"], mesh.shape["parts"] == 2)
    return jax.shard_map(
        functools.partial(on_device, pairs, block_of),
        mesh=mesh,
        in_specs=placed,
        out_specs=(P(None, ("parts", "blk")), P(("parts", "blk"))),
        check_vma=False,
    )
```

```python
import functools
import math

import jax
import jax.numpy as jnp
import numpy as np
from jax import lax
from jax.experimental import pallas as pl
from jax.experimental.pallas import tpu as pltpu
from jax.sharding import PartitionSpec as P

NEG_START = -1e30
LOG2E = math.log2(math.e)
SUBLANES = 8
LANES = 128
META_ROWS = 16
VMEM_LIMIT = 40 * 1024 * 1024


def plan(size, grid):
    chips = size // 2

    def ring(place):
        if not grid:
            return place
        return jnp.where(place < chips // 2, 2 * place, 2 * (chips - 1 - place) + 1)

    def place_of(chip):
        if not grid:
            return chip
        return jnp.where(chip % 2 == 0, chip // 2, chips - 1 - chip // 2)

    def beside(device, by):
        return ring((place_of(device // 2) + by + chips) % chips) * 2 + (device + by) % 2

    def block_of(device, step):
        if step == 0:
            return device
        stream, hop = (step - 1) % 2, (step - 1) // 2
        way = 1 - 2 * ((device + 1 + stream + hop) % 2)
        return beside(device, -way * (hop + 1))

    devices = np.arange(size)
    with jax.ensure_compile_time_eval():
        targets = [np.asarray(beside(devices, 1 - 2 * ((devices + parity) % 2))).tolist() for parity in range(2)]
    return [list(enumerate(target)) for target in targets], block_of


def joined(parts, axis):
    return parts[0] if len(parts) == 1 else jnp.concatenate(parts, axis=axis)


def row(values):
    return values.reshape(1, values.shape[-1])


def pack_kernel(params_hbm, class_hbm, evolved_hbm, upper_ref, lower_ref, params_ref, class_ref, arrived):
    rows, size = evolved_hbm.shape
    panels = size // LANES
    copies = [
        pltpu.make_async_copy(params_hbm, params_ref, arrived.at[0]),
        pltpu.make_async_copy(class_hbm, class_ref, arrived.at[1]),
    ]
    for i in range(panels):
        half = panels // 2
        panel = (upper_ref if i < half else lower_ref).at[pl.ds(i % half * rows, rows), :]
        source = evolved_hbm.at[:, pl.ds(i * LANES, LANES)]
        copies.append(pltpu.make_async_copy(source, panel, arrived.at[i + 2]))
    for copy in copies:
        copy.start()
    for copy in copies[:2]:
        copy.wait()
    params = params_ref[...].astype(jnp.float32)
    classes = row(class_ref[...]).astype(jnp.float32)
    rest = jnp.broadcast_to(classes, (META_ROWS - params.shape[0], classes.shape[1]))
    upper_ref[panels // 2 * rows :, :] = jnp.concatenate([params, rest], axis=0).astype(upper_ref.dtype)
    for copy in copies[2:]:
        copy.wait()


def norms(observed):
    rows, size = observed.shape
    sums = jnp.zeros((rows, LANES), jnp.float32)
    for i in range(size // LANES):
        panel = observed[:, i * LANES : (i + 1) * LANES].astype(jnp.float32)
        sums += panel * panel
    return jnp.sum(sums.T, axis=0, keepdims=True)


def prepare_kernel(
    block_of, at_ref, pattern_hbm, class_hbm, sharp_hbm, observed_hbm,
    own_ref, sib_ref, observed_ref, pattern_ref, class_ref, sharp_ref, arrived,
):
    sources = (pattern_hbm, class_hbm, sharp_hbm, observed_hbm)
    targets = (pattern_ref, class_ref, sharp_ref, observed_ref)
    copies = [
        pltpu.make_async_copy(source, target, arrived.at[i])
        for i, (source, target) in enumerate(zip(sources, targets))
    ]
    for copy in copies:
        copy.start()
    for copy in copies[:3]:
        copy.wait()
    tiles, devices = pattern_ref.shape
    tile = class_ref.shape[0] // tiles
    classes = row(class_ref[...]).astype(jnp.float32)
    scale = row(sharp_ref[...]) * (2.0 * LOG2E)
    for out_ref, device in ((own_ref, at_ref[0]), (sib_ref, at_ref[0] ^ 1)):
        for step in range(devices // 2):
            block = block_of(device, step)
            opened = [
                jnp.where(pattern_ref[i, block] == 1, classes[:, i * tile : (i + 1) * tile], -1.0) for i in range(tiles)
            ]
            out_ref[step : step + 1, :] = jnp.concatenate(opened, axis=1)
        out_ref[devices // 2 : devices // 2 + 1, :] = scale
    copies[3].wait()
    own_ref[devices // 2 + 1 : devices // 2 + 2, :] = norms(observed_ref[...])
    sib_ref[devices // 2 + 1 : devices // 2 + 2, :] = scale


def absorb_kernel(steps, count, first, observed_ref, aux_ref, *refs):
    count_refs = 2 * len(steps)
    packet_refs, out_ref = list(zip(refs[:count_refs:2], refs[1:count_refs:2])), refs[-1]
    panels = observed_ref.shape[1] // LANES
    half = panels // 2
    blocks = [
        jnp.concatenate([ref[i * count : (i + 1) * count, :] for ref in both for i in range(half)], axis=1)
        for both in packet_refs
    ]
    inner = lax.dot_general(
        joined(blocks, 0), observed_ref[...], (((1,), (1,)), ((), ())), preferred_element_type=jnp.float32
    )
    metas = [upper[half * count :, :] for upper, _ in packet_refs]
    after_steps = aux_ref.shape[0] - 2
    scale = aux_ref[after_steps : after_steps + 1, :]
    if first:
        top = jnp.full(scale.shape, NEG_START, jnp.float32)
    else:
        state_ref = refs[count_refs]
        top = old = state_ref[0:1, :]
    scores = []
    for i, (step, block, meta) in enumerate(zip(steps, blocks, metas)):
        wide = block.astype(jnp.float32)
        half_square = 0.5 * jnp.sum(wide * wide, axis=1, keepdims=True)
        classes = meta[META_ROWS // 2 :].astype(jnp.float32)
        column = jnp.concatenate([classes] * (count // SUBLANES), axis=0).T[:, 0:1]
        active = column == aux_ref[step : step + 1, :]
        score = jnp.where(active, inner[i * count : (i + 1) * count] - half_square, -jnp.inf)
        top = jnp.maximum(top, jnp.max(score, axis=0, keepdims=True))
        scores.append(score)
    weights = [jnp.exp2((score - top) * scale) for score in scores]
    total = sum(jnp.sum(weight, axis=0, keepdims=True) for weight in weights)
    sums = lax.dot_general(
        joined(metas, 1), joined([weight.astype(jnp.bfloat16) for weight in weights], 0),
        (((1,), (0,)), ((), ())), preferred_element_type=jnp.float32,
    )[0:4]
    if not first:
        factor = jnp.exp2((old - top) * scale)
        total += state_ref[1:2, :] * factor
        sums += state_ref[2:6, :] * factor
    out_ref[0:1, :] = top
    out_ref[1:2, :] = total
    out_ref[2:6, :] = sums
    out_ref[6:8, :] = jnp.zeros_like(out_ref[6:8, :])


def finish_kernel(size, mine_ref, other_ref, aux_ref, mean_ref, evidence_ref):
    after_steps = aux_ref.shape[0] - 2
    scale = aux_ref[after_steps : after_steps + 1, :]
    top_a, top_b = mine_ref[0:1, :], other_ref[0:1, :]
    top = jnp.maximum(top_a, top_b)
    factor_a = jnp.exp2((top_a - top) * scale)
    factor_b = jnp.exp2((top_b - top) * scale)
    total = mine_ref[1:2, :] * factor_a + other_ref[1:2, :] * factor_b
    sums = mine_ref[2:6, :] * factor_a + other_ref[2:6, :] * factor_b
    mean_ref[...] = sums / total
    sharp = scale * (0.5 / LOG2E)
    evidence = sharp * (2.0 * size - aux_ref[after_steps + 1 : after_steps + 2, :] + 2.0 * top) + jnp.log(total)
    evidence_ref[...] = evidence.reshape(evidence_ref.shape)


def after(values, *earlier):
    return lax.optimization_barrier((values, earlier))[0]


def in_hbm(*arrays):
    return [pltpu.with_memory_space_constraint(array, pltpu.HBM) for array in arrays]


def on_device(pairs, block_of, observed, sharpness, obs_class, pattern, evolved, sim_params, sim_class):
    rows, size = observed.shape
    count = evolved.shape[0]
    devices = pattern.shape[1]
    steps = devices // 2
    vmem = pl.BlockSpec(memory_space=pltpu.VMEM)
    smem = pl.BlockSpec(memory_space=pltpu.SMEM)
    hbm = pl.BlockSpec(memory_space=pltpu.HBM)
    compiler_params = pltpu.CompilerParams(vmem_limit_bytes=VMEM_LIMIT)
    f32 = jnp.float32
    core = [(i, i ^ 1) for i in range(devices)]
    at = lax.axis_index("blk").astype(jnp.int32).reshape(1)

    packet = pl.pallas_call(
        pack_kernel,
        out_shape=[
            jax.ShapeDtypeStruct((count * size // LANES // 2 + rest, LANES), evolved.dtype) for rest in (META_ROWS, 0)
        ],
        in_specs=[hbm] * 3,
        out_specs=[vmem] * 2,
        scratch_shapes=[
            pltpu.VMEM(sim_params.shape, sim_params.dtype),
            pltpu.VMEM(sim_class.shape, sim_class.dtype),
            pltpu.SemaphoreType.DMA((size // LANES + 2,)),
        ],
        compiler_params=compiler_params,
        name="pack",
    )(*in_hbm(sim_params, sim_class, evolved))
    packets = [packet]
    moving = [packet, packet]

    def send(step):
        kind = step % 2
        moving[kind] = [lax.ppermute(part, "blk", pairs[(kind + step // 2) % 2]) for part in moving[kind]]
        packets.append(moving[kind])

    send(0)
    own_aux, sib_aux, observed_own = pl.pallas_call(
        functools.partial(prepare_kernel, block_of),
        out_shape=(
            jax.ShapeDtypeStruct((steps + 2, rows), f32),
            jax.ShapeDtypeStruct((steps + 2, rows), f32),
            jax.ShapeDtypeStruct(observed.shape, observed.dtype),
        ),
        in_specs=[smem] + [hbm] * 4,
        out_specs=(vmem,) * 3,
        scratch_shapes=[
            pltpu.SMEM(pattern.shape, pattern.dtype),
            pltpu.VMEM(obs_class.shape, obs_class.dtype),
            pltpu.VMEM(sharpness.shape, sharpness.dtype),
            pltpu.SemaphoreType.DMA((4,)),
        ],
        compiler_params=compiler_params,
        cost_estimate=pl.CostEstimate(flops=8 * rows * size, bytes_accessed=4 * rows * size, transcendentals=0),
        name="prepare",
    )(after(at, packet), *in_hbm(pattern, obs_class, sharpness, observed))
    observed_sib = lax.ppermute(observed, "blk", core)
    sib_aux = lax.ppermute(sib_aux, "blk", core)
    moving[1] = after(moving[1], own_aux)
    send(1)

    def absorb(work, half, state):
        observed_half, aux = (observed_sib, sib_aux) if half else (observed_own, own_aux)
        before = () if state is None else (state,)
        return pl.pallas_call(
            functools.partial(absorb_kernel, work, count, state is None),
            out_shape=jax.ShapeDtypeStruct((SUBLANES, rows), f32),
            in_specs=[vmem] * (2 + 2 * len(work) + len(before)),
            out_specs=vmem,
            compiler_params=compiler_params,
            cost_estimate=pl.CostEstimate(
                flops=2 * len(work) * rows * count * size,
                bytes_accessed=2 * (rows + len(work) * count) * size,
                transcendentals=len(work) * rows * count,
            ),
            name="absorb",
        )(observed_half, aux, *(part for i in work for part in packets[i]), *before)

    works = [[] for _ in range(steps)]
    for block in range(1, steps - 2, 2):
        pair = (block - 1, block)
        works[block - 1].append((pair, 0))
        works[block if block < steps - 3 else block - 1].append((pair, 1))
    works[steps - 3] += [((steps - 2,), 0), ((steps - 2,), 1)]
    works[steps - 2] += [((steps - 1,), 1), ((steps - 1,), 0)]
    states = [None, None]
    done = []
    for step in range(steps - 1):
        ahead = step + 2
        if ahead < steps - 1:
            if done:
                moving[ahead % 2] = [after(part, done[-1]) for part in moving[ahead % 2]]
            send(ahead)
        last = step == steps - 2
        if step >= steps - 3:
            packets[step + 1] = after(packets[step + 1], states[0], states[1])
        for work, half in works[step]:
            states[half] = absorb(work, half, states[half])
            done.append(states[half])
            if last and half == 1:
                other = lax.ppermute(states[1], "blk", core)
    mean, evidence = pl.pallas_call(
        functools.partial(finish_kernel, size),
        out_shape=(jax.ShapeDtypeStruct((sim_params.shape[0], rows), f32), jax.ShapeDtypeStruct((rows,), f32)),
        in_specs=[vmem] * 3,
        out_specs=(vmem,) * 2,
        compiler_params=compiler_params,
        name="finish",
    )(states[0], other, own_aux)
    return mean, evidence


def solution(mesh):
    placed = (
        P(("parts", "blk"), None),
        P(("parts", "blk")),
        P(("parts", "blk")),
        P(("parts", "blk"), None),
        P(("parts", "blk"), None),
        P(None, ("parts", "blk")),
        P(("parts", "blk")),
    )
    pairs, block_of = plan(mesh.shape["blk"], mesh.shape["parts"] == 2)
    return jax.shard_map(
        functools.partial(on_device, pairs, block_of),
        mesh=mesh,
        in_specs=placed,
        out_specs=(P(None, ("parts", "blk")), P(("parts", "blk"))),
        check_vma=False,
    )
```

```python
import functools
import math

import jax
import jax.numpy as jnp
import numpy as np
from jax import lax
from jax.experimental import pallas as pl
from jax.experimental.pallas import tpu as pltpu
from jax.sharding import PartitionSpec as P

NEG_START = -1e30
LOG2E = math.log2(math.e)
SUBLANES = 8
LANES = 128
META_ROWS = 16
VMEM_LIMIT = 40 * 1024 * 1024


def plan(size, grid):
    chips = size // 2

    def ring(place):
        if not grid:
            return place
        return jnp.where(place < chips // 2, 2 * place, 2 * (chips - 1 - place) + 1)

    def place_of(chip):
        if not grid:
            return chip
        return jnp.where(chip % 2 == 0, chip // 2, chips - 1 - chip // 2)

    def beside(device, by):
        return ring((place_of(device // 2) + by + chips) % chips) * 2 + (device + by) % 2

    def block_of(device, step):
        if step == 0:
            return device
        stream, hop = (step - 1) % 2, (step - 1) // 2
        way = 1 - 2 * ((device + 1 + stream + hop) % 2)
        return beside(device, -way * (hop + 1))

    devices = np.arange(size)
    with jax.ensure_compile_time_eval():
        targets = [np.asarray(beside(devices, 1 - 2 * ((devices + parity) % 2))).tolist() for parity in range(2)]
    return [list(enumerate(target)) for target in targets], block_of


def joined(parts, axis):
    return parts[0] if len(parts) == 1 else jnp.concatenate(parts, axis=axis)


def row(values):
    return values.reshape(1, values.shape[-1])


def pack_kernel(params_hbm, class_hbm, evolved_hbm, upper_ref, lower_ref, params_ref, class_ref, arrived):
    rows, size = evolved_hbm.shape
    panels = size // LANES
    copies = [
        pltpu.make_async_copy(params_hbm, params_ref, arrived.at[0]),
        pltpu.make_async_copy(class_hbm, class_ref, arrived.at[1]),
    ]
    for i in range(panels):
        half = panels // 2
        panel = (upper_ref if i < half else lower_ref).at[pl.ds(i % half * rows, rows), :]
        source = evolved_hbm.at[:, pl.ds(i * LANES, LANES)]
        copies.append(pltpu.make_async_copy(source, panel, arrived.at[i + 2]))
    for copy in copies:
        copy.start()
    for copy in copies[:2]:
        copy.wait()
    params = params_ref[...].astype(jnp.float32)
    classes = row(class_ref[...]).astype(jnp.float32)
    rest = jnp.broadcast_to(classes, (META_ROWS - params.shape[0], classes.shape[1]))
    upper_ref[panels // 2 * rows :, :] = jnp.concatenate([params, rest], axis=0).astype(upper_ref.dtype)
    for copy in copies[2:]:
        copy.wait()


def norms(observed):
    rows, size = observed.shape
    sums = jnp.zeros((rows, LANES), jnp.float32)
    for i in range(size // LANES):
        panel = observed[:, i * LANES : (i + 1) * LANES].astype(jnp.float32)
        sums += panel * panel
    return jnp.sum(sums.T, axis=0, keepdims=True)


def prepare_kernel(
    block_of, at_ref, pattern_hbm, class_hbm, sharp_hbm, observed_hbm,
    own_ref, sib_ref, observed_ref, pattern_ref, class_ref, sharp_ref, arrived,
):
    sources = (pattern_hbm, class_hbm, sharp_hbm, observed_hbm)
    targets = (pattern_ref, class_ref, sharp_ref, observed_ref)
    copies = [
        pltpu.make_async_copy(source, target, arrived.at[i])
        for i, (source, target) in enumerate(zip(sources, targets))
    ]
    for copy in copies:
        copy.start()
    for copy in copies[:3]:
        copy.wait()
    tiles, devices = pattern_ref.shape
    tile = class_ref.shape[0] // tiles
    classes = row(class_ref[...]).astype(jnp.float32)
    scale = row(sharp_ref[...]) * (2.0 * LOG2E)
    for out_ref, device in ((own_ref, at_ref[0]), (sib_ref, at_ref[0] ^ 1)):
        for step in range(devices // 2):
            block = block_of(device, step)
            opened = [
                jnp.where(pattern_ref[i, block] == 1, classes[:, i * tile : (i + 1) * tile], -1.0) for i in range(tiles)
            ]
            out_ref[step : step + 1, :] = jnp.concatenate(opened, axis=1)
        out_ref[devices // 2 : devices // 2 + 1, :] = scale
    copies[3].wait()


def absorb_kernel(steps, count, first, with_norms, observed_ref, aux_ref, *refs):
    count_refs = 2 * len(steps)
    packet_refs, out_ref = list(zip(refs[:count_refs:2], refs[1:count_refs:2])), refs[-1]
    panels = observed_ref.shape[1] // LANES
    half = panels // 2
    blocks = [
        jnp.concatenate([ref[i * count : (i + 1) * count, :] for ref in both for i in range(half)], axis=1)
        for both in packet_refs
    ]
    inner = lax.dot_general(
        joined(blocks, 0), observed_ref[...], (((1,), (1,)), ((), ())), preferred_element_type=jnp.float32
    )
    metas = [upper[half * count :, :] for upper, _ in packet_refs]
    after_steps = aux_ref.shape[0] - 1
    scale = aux_ref[after_steps : after_steps + 1, :]
    if first:
        top = jnp.full(scale.shape, NEG_START, jnp.float32)
    else:
        state_ref = refs[count_refs]
        top = old = state_ref[0:1, :]
    scores = []
    for i, (step, block, meta) in enumerate(zip(steps, blocks, metas)):
        wide = block.astype(jnp.float32)
        half_square = 0.5 * jnp.sum(wide * wide, axis=1, keepdims=True)
        classes = meta.astype(jnp.float32)[META_ROWS // 2 :]
        column = jnp.concatenate([classes] * (count // SUBLANES), axis=0).T[:, 0:1]
        active = column == aux_ref[step : step + 1, :]
        score = jnp.where(active, inner[i * count : (i + 1) * count] - half_square, -jnp.inf)
        top = jnp.maximum(top, jnp.max(score, axis=0, keepdims=True))
        scores.append(score)
    weights = [jnp.exp2((score - top) * scale) for score in scores]
    total = sum(jnp.sum(weight, axis=0, keepdims=True) for weight in weights)
    sums = lax.dot_general(
        joined(metas, 1), joined([weight.astype(jnp.bfloat16) for weight in weights], 0),
        (((1,), (0,)), ((), ())), preferred_element_type=jnp.float32,
    )[0:4]
    if not first:
        factor = jnp.exp2((old - top) * scale)
        total += state_ref[1:2, :] * factor
        sums += state_ref[2:6, :] * factor
    out_ref[0:1, :] = top
    out_ref[1:2, :] = total
    out_ref[2:6, :] = sums
    if with_norms:
        out_ref[6:8, :] = jnp.broadcast_to(norms(observed_ref[...]), out_ref[6:8, :].shape)
    else:
        out_ref[6:8, :] = jnp.zeros_like(out_ref[6:8, :]) if first else state_ref[6:8, :]


def finish_kernel(size, mine_ref, other_ref, aux_ref, mean_ref, evidence_ref):
    after_steps = aux_ref.shape[0] - 1
    scale = aux_ref[after_steps : after_steps + 1, :]
    top_a, top_b = mine_ref[0:1, :], other_ref[0:1, :]
    top = jnp.maximum(top_a, top_b)
    factor_a = jnp.exp2((top_a - top) * scale)
    factor_b = jnp.exp2((top_b - top) * scale)
    total = mine_ref[1:2, :] * factor_a + other_ref[1:2, :] * factor_b
    sums = mine_ref[2:6, :] * factor_a + other_ref[2:6, :] * factor_b
    mean_ref[...] = sums / total
    sharp = scale * (0.5 / LOG2E)
    evidence = sharp * (2.0 * size - mine_ref[6:7, :] + 2.0 * top) + jnp.log(total)
    evidence_ref[...] = evidence.reshape(evidence_ref.shape)


def after(values, *earlier):
    return lax.optimization_barrier((values, earlier))[0]


def in_hbm(*arrays):
    return [pltpu.with_memory_space_constraint(array, pltpu.HBM) for array in arrays]


def on_device(pairs, block_of, observed, sharpness, obs_class, pattern, evolved, sim_params, sim_class):
    rows, size = observed.shape
    count = evolved.shape[0]
    devices = pattern.shape[1]
    steps = devices // 2
    vmem = pl.BlockSpec(memory_space=pltpu.VMEM)
    smem = pl.BlockSpec(memory_space=pltpu.SMEM)
    hbm = pl.BlockSpec(memory_space=pltpu.HBM)
    compiler_params = pltpu.CompilerParams(vmem_limit_bytes=VMEM_LIMIT)
    f32 = jnp.float32
    core = [(i, i ^ 1) for i in range(devices)]
    at = lax.axis_index("blk").astype(jnp.int32).reshape(1)

    packet = pl.pallas_call(
        pack_kernel,
        out_shape=[
            jax.ShapeDtypeStruct((count * size // LANES // 2 + rest, LANES), evolved.dtype) for rest in (META_ROWS, 0)
        ],
        in_specs=[hbm] * 3,
        out_specs=[vmem] * 2,
        scratch_shapes=[
            pltpu.VMEM(sim_params.shape, sim_params.dtype),
            pltpu.VMEM(sim_class.shape, sim_class.dtype),
            pltpu.SemaphoreType.DMA((size // LANES + 2,)),
        ],
        compiler_params=compiler_params,
        name="pack",
    )(*in_hbm(sim_params, sim_class, evolved))
    packets = [packet]
    moving = [packet, packet]

    def send(step):
        kind = step % 2
        moving[kind] = [lax.ppermute(part, "blk", pairs[(kind + step // 2) % 2]) for part in moving[kind]]
        packets.append(moving[kind])

    send(0)
    own_aux, sib_aux, observed_own = pl.pallas_call(
        functools.partial(prepare_kernel, block_of),
        out_shape=(
            jax.ShapeDtypeStruct((steps + 1, rows), f32),
            jax.ShapeDtypeStruct((steps + 1, rows), f32),
            jax.ShapeDtypeStruct(observed.shape, observed.dtype),
        ),
        in_specs=[smem] + [hbm] * 4,
        out_specs=(vmem,) * 3,
        scratch_shapes=[
            pltpu.SMEM(pattern.shape, pattern.dtype),
            pltpu.VMEM(obs_class.shape, obs_class.dtype),
            pltpu.VMEM(sharpness.shape, sharpness.dtype),
            pltpu.SemaphoreType.DMA((4,)),
        ],
        compiler_params=compiler_params,
        cost_estimate=pl.CostEstimate(flops=8 * rows * size, bytes_accessed=4 * rows * size, transcendentals=0),
        name="prepare",
    )(after(at, packet), *in_hbm(pattern, obs_class, sharpness, observed))
    observed_sib = lax.ppermute(observed, "blk", core)
    sib_aux = lax.ppermute(sib_aux, "blk", core)
    moving[1] = after(moving[1], own_aux)
    send(1)

    def absorb(work, half, state):
        observed_half, aux = (observed_sib, sib_aux) if half else (observed_own, own_aux)
        before = () if state is None else (state,)
        return pl.pallas_call(
            functools.partial(absorb_kernel, work, count, state is None, half == 0 and work == (steps - 2,)),
            out_shape=jax.ShapeDtypeStruct((SUBLANES, rows), f32),
            in_specs=[vmem] * (2 + 2 * len(work) + len(before)),
            out_specs=vmem,
            compiler_params=compiler_params,
            cost_estimate=pl.CostEstimate(
                flops=2 * len(work) * rows * count * size,
                bytes_accessed=2 * (rows + len(work) * count) * size,
                transcendentals=len(work) * rows * count,
            ),
            name="absorb",
        )(observed_half, aux, *(part for i in work for part in packets[i]), *before)

    works = [[] for _ in range(steps)]
    for block in range(1, steps - 2, 2):
        pair = (block - 1, block)
        works[block - 1].append((pair, 0))
        if block < steps - 3:
            works[block].append((pair, 1))
    works[steps - 3] += [((steps - 2,), 0), ((*pair, steps - 2), 1)]
    works[steps - 2] += [((steps - 1,), 1), ((steps - 1,), 0)]
    states = [None, None]
    done = []
    for step in range(steps - 1):
        ahead = step + 2
        if ahead < steps - 1:
            if done:
                moving[ahead % 2] = [after(part, done[-1]) for part in moving[ahead % 2]]
            send(ahead)
        last = step == steps - 2
        if step >= steps - 3:
            packets[step + 1] = after(packets[step + 1], states[0], states[1])
        for work, half in works[step]:
            states[half] = absorb(work, half, states[half])
            done.append(states[half])
            if last and half == 1:
                other = lax.ppermute(states[1], "blk", core)
    mean, evidence = pl.pallas_call(
        functools.partial(finish_kernel, size),
        out_shape=(jax.ShapeDtypeStruct((sim_params.shape[0], rows), f32), jax.ShapeDtypeStruct((rows,), f32)),
        in_specs=[vmem] * 3,
        out_specs=(vmem,) * 2,
        compiler_params=compiler_params,
        name="finish",
    )(states[0], other, own_aux)
    return mean, evidence


def solution(mesh):
    placed = (
        P(("parts", "blk"), None),
        P(("parts", "blk")),
        P(("parts", "blk")),
        P(("parts", "blk"), None),
        P(("parts", "blk"), None),
        P(None, ("parts", "blk")),
        P(("parts", "blk")),
    )
    pairs, block_of = plan(mesh.shape["blk"], mesh.shape["parts"] == 2)
    return jax.shard_map(
        functools.partial(on_device, pairs, block_of),
        mesh=mesh,
        in_specs=placed,
        out_specs=(P(None, ("parts", "blk")), P(("parts", "blk"))),
        check_vma=False,
    )
```

```python
import functools
import math

import jax
import jax.numpy as jnp
import numpy as np
from jax import lax
from jax.experimental import pallas as pl
from jax.experimental.pallas import tpu as pltpu
from jax.sharding import PartitionSpec as P

NEG_START = -1e30
LOG2E = math.log2(math.e)
SUBLANES = 8
LANES = 128
META_ROWS = 16
VMEM_LIMIT = 40 * 1024 * 1024


def plan(size, grid):
    chips = size // 2

    def ring(place):
        if not grid:
            return place
        return jnp.where(place < chips // 2, 2 * place, 2 * (chips - 1 - place) + 1)

    def place_of(chip):
        if not grid:
            return chip
        return jnp.where(chip % 2 == 0, chip // 2, chips - 1 - chip // 2)

    def beside(device, by):
        return ring((place_of(device // 2) + by + chips) % chips) * 2 + (device + by) % 2

    def block_of(device, step):
        if step == 0:
            return device
        stream, hop = (step - 1) % 2, (step - 1) // 2
        way = 1 - 2 * ((device + 1 + stream + hop) % 2)
        return beside(device, -way * (hop + 1))

    devices = np.arange(size)
    with jax.ensure_compile_time_eval():
        targets = [np.asarray(beside(devices, 1 - 2 * ((devices + parity) % 2))).tolist() for parity in range(2)]
    return [list(enumerate(target)) for target in targets], block_of


def joined(parts, axis):
    return parts[0] if len(parts) == 1 else jnp.concatenate(parts, axis=axis)


def row(values):
    return values.reshape(1, values.shape[-1])


def pack_kernel(params_hbm, class_hbm, evolved_hbm, upper_ref, lower_ref, params_ref, class_ref, arrived):
    rows, size = evolved_hbm.shape
    panels = size // LANES
    copies = [
        pltpu.make_async_copy(params_hbm, params_ref, arrived.at[0]),
        pltpu.make_async_copy(class_hbm, class_ref, arrived.at[1]),
    ]
    for i in range(panels):
        half = panels // 2
        panel = (upper_ref if i < half else lower_ref).at[pl.ds(i % half * rows, rows), :]
        source = evolved_hbm.at[:, pl.ds(i * LANES, LANES)]
        copies.append(pltpu.make_async_copy(source, panel, arrived.at[i + 2]))
    for copy in copies:
        copy.start()
    for copy in copies[:2]:
        copy.wait()
    params = params_ref[...].astype(jnp.float32)
    classes = row(class_ref[...]).astype(jnp.float32)
    rest = jnp.broadcast_to(classes, (META_ROWS - params.shape[0], classes.shape[1]))
    upper_ref[panels // 2 * rows :, :] = jnp.concatenate([params, rest], axis=0).astype(upper_ref.dtype)
    for copy in copies[2:]:
        copy.wait()


def norms(observed):
    rows, size = observed.shape
    sums = jnp.zeros((rows, LANES), jnp.float32)
    for i in range(size // LANES):
        panel = observed[:, i * LANES : (i + 1) * LANES].astype(jnp.float32)
        sums += panel * panel
    return jnp.sum(sums.T, axis=0, keepdims=True)


def prepare_kernel(
    block_of, at_ref, pattern_hbm, class_hbm, sharp_hbm, observed_hbm,
    own_ref, sib_ref, observed_ref, pattern_ref, class_ref, sharp_ref, arrived,
):
    sources = (pattern_hbm, class_hbm, sharp_hbm, observed_hbm)
    targets = (pattern_ref, class_ref, sharp_ref, observed_ref)
    copies = [
        pltpu.make_async_copy(source, target, arrived.at[i])
        for i, (source, target) in enumerate(zip(sources, targets))
    ]
    for copy in copies:
        copy.start()
    for copy in copies[:3]:
        copy.wait()
    tiles, devices = pattern_ref.shape
    tile = class_ref.shape[0] // tiles
    classes = row(class_ref[...]).astype(jnp.float32)
    scale = row(sharp_ref[...]) * (2.0 * LOG2E)
    for out_ref, device in ((own_ref, at_ref[0]), (sib_ref, at_ref[0] ^ 1)):
        for step in range(devices // 2):
            block = block_of(device, step)
            opened = [
                jnp.where(pattern_ref[i, block] == 1, classes[:, i * tile : (i + 1) * tile], -1.0) for i in range(tiles)
            ]
            out_ref[step : step + 1, :] = jnp.concatenate(opened, axis=1)
        out_ref[devices // 2 : devices // 2 + 1, :] = scale
    copies[3].wait()


def absorb_kernel(steps, count, first, with_norms, observed_ref, aux_ref, *refs):
    count_refs = 2 * len(steps)
    packet_refs, out_ref = list(zip(refs[:count_refs:2], refs[1:count_refs:2])), refs[-1]
    panels = observed_ref.shape[1] // LANES
    half = panels // 2
    blocks = [
        jnp.concatenate([ref[i * count : (i + 1) * count, :] for ref in both for i in range(half)], axis=1)
        for both in packet_refs
    ]
    inner = lax.dot_general(
        joined(blocks, 0), observed_ref[...], (((1,), (1,)), ((), ())), preferred_element_type=jnp.float32
    )
    metas = [upper[half * count :, :] for upper, _ in packet_refs]
    after_steps = aux_ref.shape[0] - 1
    scale = aux_ref[after_steps : after_steps + 1, :]
    if first:
        top = jnp.full(scale.shape, NEG_START, jnp.float32)
    else:
        state_ref = refs[count_refs]
        top = old = state_ref[0:1, :]
    scores = []
    for i, (step, block, meta) in enumerate(zip(steps, blocks, metas)):
        wide = block.astype(jnp.float32)
        half_square = 0.5 * jnp.sum(wide * wide, axis=1, keepdims=True)
        classes = meta.astype(jnp.float32)[META_ROWS // 2 :]
        column = jnp.concatenate([classes] * (count // SUBLANES), axis=0).T[:, 0:1]
        active = column == aux_ref[step : step + 1, :]
        score = jnp.where(active, inner[i * count : (i + 1) * count] - half_square, -jnp.inf)
        top = jnp.maximum(top, jnp.max(score, axis=0, keepdims=True))
        scores.append(score)
    weights = [jnp.exp2((score - top) * scale) for score in scores]
    total = sum(jnp.sum(weight, axis=0, keepdims=True) for weight in weights)
    sums = lax.dot_general(
        joined(metas, 1), joined([weight.astype(jnp.bfloat16) for weight in weights], 0),
        (((1,), (0,)), ((), ())), preferred_element_type=jnp.float32,
    )[0:4]
    if not first:
        factor = jnp.exp2((old - top) * scale)
        total += state_ref[1:2, :] * factor
        sums += state_ref[2:6, :] * factor
    out_ref[0:1, :] = top
    out_ref[1:2, :] = total
    out_ref[2:6, :] = sums
    if with_norms:
        out_ref[6:8, :] = jnp.broadcast_to(norms(observed_ref[...]), out_ref[6:8, :].shape)
    else:
        out_ref[6:8, :] = jnp.zeros_like(out_ref[6:8, :]) if first else state_ref[6:8, :]


def finish_kernel(size, mine_ref, other_ref, aux_ref, mean_ref, evidence_ref):
    after_steps = aux_ref.shape[0] - 1
    scale = aux_ref[after_steps : after_steps + 1, :]
    top_a, top_b = mine_ref[0:1, :], other_ref[0:1, :]
    top = jnp.maximum(top_a, top_b)
    factor_a = jnp.exp2((top_a - top) * scale)
    factor_b = jnp.exp2((top_b - top) * scale)
    total = mine_ref[1:2, :] * factor_a + other_ref[1:2, :] * factor_b
    sums = mine_ref[2:6, :] * factor_a + other_ref[2:6, :] * factor_b
    mean_ref[...] = sums / total
    sharp = scale * (0.5 / LOG2E)
    evidence = sharp * (2.0 * size - mine_ref[6:7, :] + 2.0 * top) + jnp.log(total)
    evidence_ref[...] = evidence.reshape(evidence_ref.shape)


def after(values, *earlier):
    return lax.optimization_barrier((values, earlier))[0]


def in_hbm(*arrays):
    return [pltpu.with_memory_space_constraint(array, pltpu.HBM) for array in arrays]


def on_device(pairs, block_of, observed, sharpness, obs_class, pattern, evolved, sim_params, sim_class):
    rows, size = observed.shape
    count = evolved.shape[0]
    devices = pattern.shape[1]
    steps = devices // 2
    vmem = pl.BlockSpec(memory_space=pltpu.VMEM)
    smem = pl.BlockSpec(memory_space=pltpu.SMEM)
    hbm = pl.BlockSpec(memory_space=pltpu.HBM)
    compiler_params = pltpu.CompilerParams(vmem_limit_bytes=VMEM_LIMIT)
    f32 = jnp.float32
    core = [(i, i ^ 1) for i in range(devices)]
    at = lax.axis_index("blk").astype(jnp.int32).reshape(1)

    packet = pl.pallas_call(
        pack_kernel,
        out_shape=[
            jax.ShapeDtypeStruct((count * size // LANES // 2 + rest, LANES), evolved.dtype) for rest in (META_ROWS, 0)
        ],
        in_specs=[hbm] * 3,
        out_specs=[vmem] * 2,
        scratch_shapes=[
            pltpu.VMEM(sim_params.shape, sim_params.dtype),
            pltpu.VMEM(sim_class.shape, sim_class.dtype),
            pltpu.SemaphoreType.DMA((size // LANES + 2,)),
        ],
        compiler_params=compiler_params,
        name="pack",
    )(*in_hbm(sim_params, sim_class, evolved))
    packets = [packet]
    moving = [packet, packet]

    def send(step):
        kind = step % 2
        moving[kind] = [lax.ppermute(part, "blk", pairs[(kind + step // 2) % 2]) for part in moving[kind]]
        packets.append(moving[kind])

    send(0)
    own_aux, sib_aux, observed_own = pl.pallas_call(
        functools.partial(prepare_kernel, block_of),
        out_shape=(
            jax.ShapeDtypeStruct((steps + 1, rows), f32),
            jax.ShapeDtypeStruct((steps + 1, rows), f32),
            jax.ShapeDtypeStruct(observed.shape, observed.dtype),
        ),
        in_specs=[smem] + [hbm] * 4,
        out_specs=(vmem,) * 3,
        scratch_shapes=[
            pltpu.SMEM(pattern.shape, pattern.dtype),
            pltpu.VMEM(obs_class.shape, obs_class.dtype),
            pltpu.VMEM(sharpness.shape, sharpness.dtype),
            pltpu.SemaphoreType.DMA((4,)),
        ],
        compiler_params=compiler_params,
        cost_estimate=pl.CostEstimate(flops=8 * rows * size, bytes_accessed=4 * rows * size, transcendentals=0),
        name="prepare",
    )(after(at, packet), *in_hbm(pattern, obs_class, sharpness, observed))
    observed_sib = lax.ppermute(after(observed, packet[0]), "blk", core)
    sib_aux = lax.ppermute(sib_aux, "blk", core)
    moving[1] = after(moving[1], own_aux)
    send(1)

    def absorb(work, half, state):
        observed_half, aux = (observed_sib, sib_aux) if half else (observed_own, own_aux)
        before = () if state is None else (state,)
        return pl.pallas_call(
            functools.partial(absorb_kernel, work, count, state is None, half == 0 and work == (steps - 2,)),
            out_shape=jax.ShapeDtypeStruct((SUBLANES, rows), f32),
            in_specs=[vmem] * (2 + 2 * len(work) + len(before)),
            out_specs=vmem,
            compiler_params=compiler_params,
            cost_estimate=pl.CostEstimate(
                flops=2 * len(work) * rows * count * size,
                bytes_accessed=2 * (rows + len(work) * count) * size,
                transcendentals=len(work) * rows * count,
            ),
            name="absorb",
        )(observed_half, aux, *(part for i in work for part in packets[i]), *before)

    works = [[] for _ in range(steps)]
    for block in range(1, steps - 2, 2):
        pair = (block - 1, block)
        works[block - 1].append((pair, 0))
        if block < steps - 3:
            works[block].append((pair, 1))
    works[steps - 3] += [((steps - 2,), 0), ((*pair, steps - 2), 1)]
    works[steps - 2] += [((steps - 1,), 1), ((steps - 1,), 0)]
    states = [None, None]
    done = []
    for step in range(steps - 1):
        ahead = step + 2
        if ahead < steps - 1:
            if done:
                moving[ahead % 2] = [after(part, done[-2 if ahead == steps - 2 and i == 0 else -1]) for i, part in enumerate(moving[ahead % 2])]
            send(ahead)
        last = step == steps - 2
        if step >= steps - 3:
            packets[step + 1] = after(packets[step + 1], states[0], states[1])
        for work, half in works[step]:
            states[half] = absorb(work, half, states[half])
            done.append(states[half])
            if last and half == 1:
                other = lax.ppermute(states[1], "blk", core)
    mean, evidence = pl.pallas_call(
        functools.partial(finish_kernel, size),
        out_shape=(jax.ShapeDtypeStruct((sim_params.shape[0], rows), f32), jax.ShapeDtypeStruct((rows,), f32)),
        in_specs=[vmem] * 3,
        out_specs=(vmem,) * 2,
        compiler_params=compiler_params,
        name="finish",
    )(states[0], other, own_aux)
    return mean, evidence


def solution(mesh):
    placed = (
        P(("parts", "blk"), None),
        P(("parts", "blk")),
        P(("parts", "blk")),
        P(("parts", "blk"), None),
        P(("parts", "blk"), None),
        P(None, ("parts", "blk")),
        P(("parts", "blk")),
    )
    pairs, block_of = plan(mesh.shape["blk"], mesh.shape["parts"] == 2)
    return jax.shard_map(
        functools.partial(on_device, pairs, block_of),
        mesh=mesh,
        in_specs=placed,
        out_specs=(P(None, ("parts", "blk")), P(("parts", "blk"))),
        check_vma=False,
    )
```

```python
import functools
import math

import jax
import jax.numpy as jnp
import numpy as np
from jax import lax
from jax.experimental import pallas as pl
from jax.experimental.pallas import tpu as pltpu
from jax.sharding import PartitionSpec as P

NEG_START = -1e30
LOG2E = math.log2(math.e)
SUBLANES = 8
LANES = 128
META_ROWS = 16
VMEM_LIMIT = 40 * 1024 * 1024


def plan(size, grid):
    chips = size // 2

    def ring(place):
        if not grid:
            return place
        return jnp.where(place < chips // 2, 2 * place, 2 * (chips - 1 - place) + 1)

    def place_of(chip):
        if not grid:
            return chip
        return jnp.where(chip % 2 == 0, chip // 2, chips - 1 - chip // 2)

    def beside(device, by):
        return ring((place_of(device // 2) + by + chips) % chips) * 2 + (device + by) % 2

    def block_of(device, step):
        if step == 0:
            return device
        stream, hop = (step - 1) % 2, (step - 1) // 2
        way = 1 - 2 * ((device + 1 + stream + hop) % 2)
        return beside(device, -way * (hop + 1))

    devices = np.arange(size)
    with jax.ensure_compile_time_eval():
        targets = [np.asarray(beside(devices, 1 - 2 * ((devices + parity) % 2))).tolist() for parity in range(2)]
    return [list(enumerate(target)) for target in targets], block_of


def joined(parts, axis):
    return parts[0] if len(parts) == 1 else jnp.concatenate(parts, axis=axis)


def row(values):
    return values.reshape(1, values.shape[-1])


def pack_kernel(params_hbm, class_hbm, evolved_hbm, upper_ref, lower_ref, params_ref, class_ref, arrived):
    rows, size = evolved_hbm.shape
    panels = size // LANES
    copies = [
        pltpu.make_async_copy(params_hbm, params_ref, arrived.at[0]),
        pltpu.make_async_copy(class_hbm, class_ref, arrived.at[1]),
    ]
    for i in range(panels):
        half = panels // 2
        panel = (upper_ref if i < half else lower_ref).at[pl.ds(i % half * rows, rows), :]
        source = evolved_hbm.at[:, pl.ds(i * LANES, LANES)]
        copies.append(pltpu.make_async_copy(source, panel, arrived.at[i + 2]))
    for copy in copies:
        copy.start()
    for copy in copies[:2]:
        copy.wait()
    params = params_ref[...].astype(jnp.float32)
    classes = row(class_ref[...]).astype(jnp.float32)
    rest = jnp.broadcast_to(classes, (META_ROWS - params.shape[0], classes.shape[1]))
    upper_ref[panels // 2 * rows :, :] = jnp.concatenate([params, rest], axis=0).astype(upper_ref.dtype)
    for copy in copies[2:]:
        copy.wait()


def norms(observed):
    rows, size = observed.shape
    sums = jnp.zeros((rows, LANES), jnp.float32)
    for i in range(size // LANES):
        panel = observed[:, i * LANES : (i + 1) * LANES].astype(jnp.float32)
        sums += panel * panel
    return jnp.sum(sums.T, axis=0, keepdims=True)


def prepare_kernel(
    block_of, at_ref, pattern_hbm, class_hbm, sharp_hbm, observed_hbm,
    own_ref, sib_ref, observed_ref, pattern_ref, class_ref, sharp_ref, arrived,
):
    sources = (pattern_hbm, class_hbm, sharp_hbm, observed_hbm)
    targets = (pattern_ref, class_ref, sharp_ref, observed_ref)
    copies = [
        pltpu.make_async_copy(source, target, arrived.at[i])
        for i, (source, target) in enumerate(zip(sources, targets))
    ]
    for copy in reversed(copies):
        copy.start()
    for copy in copies[:3]:
        copy.wait()
    tiles, devices = pattern_ref.shape
    tile = class_ref.shape[0] // tiles
    classes = row(class_ref[...]).astype(jnp.float32)
    scale = row(sharp_ref[...]) * (2.0 * LOG2E)
    for out_ref, device in ((own_ref, at_ref[0]), (sib_ref, at_ref[0] ^ 1)):
        for step in range(devices // 2):
            block = block_of(device, step)
            opened = [
                jnp.where(pattern_ref[i, block] == 1, classes[:, i * tile : (i + 1) * tile], -1.0) for i in range(tiles)
            ]
            out_ref[step : step + 1, :] = jnp.concatenate(opened, axis=1)
        out_ref[devices // 2 : devices // 2 + 1, :] = scale
    copies[3].wait()


def absorb_kernel(steps, count, first, with_norms, observed_ref, aux_ref, *refs):
    count_refs = 2 * len(steps)
    packet_refs, out_ref = list(zip(refs[:count_refs:2], refs[1:count_refs:2])), refs[-1]
    panels = observed_ref.shape[1] // LANES
    half = panels // 2
    blocks = [
        jnp.concatenate([ref[i * count : (i + 1) * count, :] for ref in both for i in range(half)], axis=1)
        for both in packet_refs
    ]
    inner = lax.dot_general(
        joined(blocks, 0), observed_ref[...], (((1,), (1,)), ((), ())), preferred_element_type=jnp.float32
    )
    metas = [upper[half * count :, :] for upper, _ in packet_refs]
    after_steps = aux_ref.shape[0] - 1
    scale = aux_ref[after_steps : after_steps + 1, :]
    if first:
        top = jnp.full(scale.shape, NEG_START, jnp.float32)
    else:
        state_ref = refs[count_refs]
        top = old = state_ref[0:1, :]
    scores = []
    for i, (step, block, meta) in enumerate(zip(steps, blocks, metas)):
        wide = block.astype(jnp.float32)
        half_square = 0.5 * jnp.sum(wide * wide, axis=1, keepdims=True)
        classes = meta.astype(jnp.float32)[META_ROWS // 2 :]
        column = jnp.concatenate([classes] * (count // SUBLANES), axis=0).T[:, 0:1]
        active = column == aux_ref[step : step + 1, :]
        score = jnp.where(active, inner[i * count : (i + 1) * count] - half_square, -jnp.inf)
        top = jnp.maximum(top, jnp.max(score, axis=0, keepdims=True))
        scores.append(score)
    weights = [jnp.exp2((score - top) * scale) for score in scores]
    total = sum(jnp.sum(weight, axis=0, keepdims=True) for weight in weights)
    sums = lax.dot_general(
        joined(metas, 1), joined([weight.astype(jnp.bfloat16) for weight in weights], 0),
        (((1,), (0,)), ((), ())), preferred_element_type=jnp.float32,
    )[0:4]
    if not first:
        factor = jnp.exp2((old - top) * scale)
        total += state_ref[1:2, :] * factor
        sums += state_ref[2:6, :] * factor
    out_ref[0:1, :] = top
    out_ref[1:2, :] = total
    out_ref[2:6, :] = sums
    if with_norms:
        out_ref[6:8, :] = jnp.broadcast_to(norms(observed_ref[...]), out_ref[6:8, :].shape)
    else:
        out_ref[6:8, :] = jnp.zeros_like(out_ref[6:8, :]) if first else state_ref[6:8, :]


def finish_kernel(size, mine_ref, other_ref, aux_ref, mean_ref, evidence_ref):
    after_steps = aux_ref.shape[0] - 1
    scale = aux_ref[after_steps : after_steps + 1, :]
    top_a, top_b = mine_ref[0:1, :], other_ref[0:1, :]
    top = jnp.maximum(top_a, top_b)
    factor_a = jnp.exp2((top_a - top) * scale)
    factor_b = jnp.exp2((top_b - top) * scale)
    total = mine_ref[1:2, :] * factor_a + other_ref[1:2, :] * factor_b
    sums = mine_ref[2:6, :] * factor_a + other_ref[2:6, :] * factor_b
    mean_ref[...] = sums / total
    sharp = scale * (0.5 / LOG2E)
    evidence = sharp * (2.0 * size - mine_ref[6:7, :] + 2.0 * top) + jnp.log(total)
    evidence_ref[...] = evidence.reshape(evidence_ref.shape)


def after(values, *earlier):
    return lax.optimization_barrier((values, earlier))[0]


def in_hbm(*arrays):
    return [pltpu.with_memory_space_constraint(array, pltpu.HBM) for array in arrays]


def on_device(pairs, block_of, observed, sharpness, obs_class, pattern, evolved, sim_params, sim_class):
    rows, size = observed.shape
    count = evolved.shape[0]
    devices = pattern.shape[1]
    steps = devices // 2
    vmem = pl.BlockSpec(memory_space=pltpu.VMEM)
    smem = pl.BlockSpec(memory_space=pltpu.SMEM)
    hbm = pl.BlockSpec(memory_space=pltpu.HBM)
    compiler_params = pltpu.CompilerParams(vmem_limit_bytes=VMEM_LIMIT)
    f32 = jnp.float32
    core = [(i, i ^ 1) for i in range(devices)]
    at = lax.axis_index("blk").astype(jnp.int32).reshape(1)

    packet = pl.pallas_call(
        pack_kernel,
        out_shape=[
            jax.ShapeDtypeStruct((count * size // LANES // 2 + rest, LANES), evolved.dtype) for rest in (META_ROWS, 0)
        ],
        in_specs=[hbm] * 3,
        out_specs=[vmem] * 2,
        scratch_shapes=[
            pltpu.VMEM(sim_params.shape, sim_params.dtype),
            pltpu.VMEM(sim_class.shape, sim_class.dtype),
            pltpu.SemaphoreType.DMA((size // LANES + 2,)),
        ],
        compiler_params=compiler_params,
        name="pack",
    )(*in_hbm(sim_params, sim_class, evolved))
    packets = [packet]
    moving = [packet, packet]

    def send(step):
        kind = step % 2
        moving[kind] = [lax.ppermute(part, "blk", pairs[(kind + step // 2) % 2]) for part in moving[kind]]
        packets.append(moving[kind])

    send(0)
    own_aux, sib_aux, observed_own = pl.pallas_call(
        functools.partial(prepare_kernel, block_of),
        out_shape=(
            jax.ShapeDtypeStruct((steps + 1, rows), f32),
            jax.ShapeDtypeStruct((steps + 1, rows), f32),
            jax.ShapeDtypeStruct(observed.shape, observed.dtype),
        ),
        in_specs=[smem] + [hbm] * 4,
        out_specs=(vmem,) * 3,
        scratch_shapes=[
            pltpu.SMEM(pattern.shape, pattern.dtype),
            pltpu.VMEM(obs_class.shape, obs_class.dtype),
            pltpu.VMEM(sharpness.shape, sharpness.dtype),
            pltpu.SemaphoreType.DMA((4,)),
        ],
        compiler_params=compiler_params,
        cost_estimate=pl.CostEstimate(flops=8 * rows * size, bytes_accessed=4 * rows * size, transcendentals=0),
        name="prepare",
    )(after(at, packet), *in_hbm(pattern, obs_class, sharpness, observed))
    observed_sib = lax.ppermute(after(observed, packet[0]), "blk", core)
    sib_aux = lax.ppermute(sib_aux, "blk", core)
    moving[1] = after(moving[1], own_aux)
    send(1)

    def absorb(work, half, state):
        observed_half, aux = (observed_sib, sib_aux) if half else (observed_own, own_aux)
        before = () if state is None else (state,)
        return pl.pallas_call(
            functools.partial(absorb_kernel, work, count, state is None, half == 0 and work == (steps - 2,)),
            out_shape=jax.ShapeDtypeStruct((SUBLANES, rows), f32),
            in_specs=[vmem] * (2 + 2 * len(work) + len(before)),
            out_specs=vmem,
            compiler_params=compiler_params,
            cost_estimate=pl.CostEstimate(
                flops=2 * len(work) * rows * count * size,
                bytes_accessed=2 * (rows + len(work) * count) * size,
                transcendentals=len(work) * rows * count,
            ),
            name="absorb",
        )(observed_half, aux, *(part for i in work for part in packets[i]), *before)

    works = [[] for _ in range(steps)]
    for block in range(1, steps - 2, 2):
        pair = (block - 1, block)
        works[block - 1].append((pair, 0))
        if block < steps - 3:
            works[block].append((pair, 1))
    works[steps - 3] += [((steps - 2,), 0), ((*pair, steps - 2), 1)]
    works[steps - 2] += [((steps - 1,), 1), ((steps - 1,), 0)]
    states = [None, None]
    done = []
    for step in range(steps - 1):
        ahead = step + 2
        if ahead < steps - 1:
            if done:
                moving[ahead % 2] = [after(part, done[-2 if ahead == steps - 2 and i == 0 else -1]) for i, part in enumerate(moving[ahead % 2])]
            send(ahead)
        last = step == steps - 2
        if step >= steps - 3:
            packets[step + 1] = after(packets[step + 1], states[0], states[1])
        for work, half in works[step]:
            states[half] = absorb(work, half, states[half])
            done.append(states[half])
            if last and half == 1:
                other = lax.ppermute(states[1], "blk", core)
    mean, evidence = pl.pallas_call(
        functools.partial(finish_kernel, size),
        out_shape=(jax.ShapeDtypeStruct((sim_params.shape[0], rows), f32), jax.ShapeDtypeStruct((rows,), f32)),
        in_specs=[vmem] * 3,
        out_specs=(vmem,) * 2,
        compiler_params=compiler_params,
        name="finish",
    )(states[0], other, own_aux)
    return mean, evidence


def solution(mesh):
    placed = (
        P(("parts", "blk"), None),
        P(("parts", "blk")),
        P(("parts", "blk")),
        P(("parts", "blk"), None),
        P(("parts", "blk"), None),
        P(None, ("parts", "blk")),
        P(("parts", "blk")),
    )
    pairs, block_of = plan(mesh.shape["blk"], mesh.shape["parts"] == 2)
    return jax.shard_map(
        functools.partial(on_device, pairs, block_of),
        mesh=mesh,
        in_specs=placed,
        out_specs=(P(None, ("parts", "blk")), P(("parts", "blk"))),
        check_vma=False,
    )
```
